32 devices in a mesh: lon: 4 (over x, core), lat: 4 (over z), dp: 2 (over y).
Axes of the slice: x: 2, y: 2, z: 4, core: 2. Of those that a mesh axis runs over, the one named last changes fastest.
Arguments:
- tokens: bfloat16 [2, 2, 32, 64, 1024], P('dp', None, 'lat', 'lon'), may hold values from -6 to 6
- norm_gain: float32 [1024], replicated, may hold values from 0.1 to 1.9
- w_qkv: bfloat16 [1024, 3072], replicated, may hold values from -8 to 8
- w_out: bfloat16 [1024, 1024], replicated, may hold values from -0.1875 to 0.1875
- obs_vectors: bfloat16 [2048, 1024], P(('lon', 'lat', 'dp')), may hold values from -6 to 6
- obs_lat: int32 [2048, 1], P(('lon', 'lat', 'dp')), may hold values from 0 to 3; in each aligned block of 64 rows (0 to 63, 64 to 127, ...) at most 24 rows name the same one
- obs_cell: int32 [2048], P(('lon', 'lat', 'dp')), may hold values from 0 to 255
- obs_count: int32 [32], P(('lon', 'lat', 'dp')), may hold values from 1 to 64, 1536 in all
- shift_offsets: int32 [2, 2], P('dp'), may hold values from 1 to 7, as said below
- cotangent: bfloat16 [2, 2, 32, 64, 1024], P('dp', None, 'lat', 'lon'), may hold values from -0.09375 to 0.09375
Outputs:
- block_out: bfloat16 [2, 2, 32, 64, 1024], P('dp', None, 'lat', 'lon')
- gradient: float32 [1024, 1024], P('lon', ('lat', 'dp'))
The draws below stay inside these ranges and needn't reach their ends.
Inputs may be any that keep to these rules, and one draw needn't show every extreme that they name: `obs_lat`: among the 64 rows of one device at most 24 name the same latitude index; some device has exactly 24 for some index. `obs_count`: some device has exactly 64 live rows. `shift_offsets`: each column takes the value 8 - 1 for some sample.
All inputs are finite; a program needn't handle non-finite values.
Results may differ from the reference program's by a relative error of at most 0.0086.
Values may be sent and summed in bfloat16 or wider, within the bound.
No kernel may reach another device: no remote copies, remote signals or barrier semaphores. Data moves between devices by JAX's collectives and lax.ppermute only.
A program may use at most 64 MiB of HBM per device.

```python
import math
import jax
import jax.numpy as jnp
import numpy as np
from jax import lax

D = 1024
HEADS = 16
WIN = 8
LEVELS = 2
LAT_DEV = 8
LON_DEV = 16
OBS_DEV = 64
BATCH = 2
LAT = 32
LON = 64
TOK_DEV = 256
ALL_TOK = 8192
OBS = 2048
CAP = 24
N_LAT = 4
N_DP = 2
DEVICES = 32


def draw_w_qkv(key, part):
    keys = jax.random.split(key, 1)
    base = jnp.clip(jax.random.normal(keys[0], (D, 3 * D), jnp.float32), -6.0, 6.0) * D ** (-0.5)
    return jnp.clip(base, -8.0, 8.0).astype(jnp.bfloat16)


def draw_shift_offsets(key, part):
    values = jax.random.randint(key, (BATCH, 2), 1, WIN, dtype=jnp.int32)
    chosen = jax.random.randint(jax.random.fold_in(key, 7), (2,), 0, BATCH, dtype=jnp.int32)
    sample_ids = jnp.arange(BATCH, dtype=jnp.int32)
    return jnp.where(sample_ids[:, None] == chosen[None, :], WIN - 1, values).astype(jnp.int32)


def touch_ends(values, rng, least, largest):
    index_at = [jax.random.randint(jax.random.fold_in(rng, axis), (), 0, length) for axis, length in enumerate(values.shape)]
    widest = values.shape.index(max(values.shape))
    next_to = index_at[:widest] + [(index_at[widest] + 1) % values.shape[widest]] + index_at[widest + 1:]
    return values.at[tuple(index_at)].set(least).at[tuple(next_to)].set(largest)


def raised(array, key, source, target, shards_of, factor):
    def block_of(dim):
        return (jnp.arange(array.shape[dim]) // (array.shape[dim] // shards_of)).reshape((-1,) + (1,) * (array.ndim - 1 - dim))

    near = jax.random.permutation(key, shards_of)[block_of(target)]
    second = (block_of(target) + shards_of // 2) % shards_of
    return jnp.where((block_of(source) == near) | (block_of(source) == second), factor * array, array)


def shard_levels(key, shape, cuts, low, largest):
    factor_of, own = 1.0, jax.random.fold_in(key, 6)
    for axis_at, blocks in cuts:
        steps = jnp.exp(jax.random.uniform(jax.random.fold_in(own, axis_at), (blocks,), jnp.float32, low / len(cuts), largest / len(cuts)))
        factor_of = factor_of * jnp.repeat(steps, shape[axis_at] // blocks).reshape([-1 if axis == axis_at else 1 for axis in range(len(shape))])
    return factor_of


def split_up(number_of, total, bound, slope):
    loads = [(1 << 20) // math.isqrt(standing ** slope) + 1 for standing in range(2, number_of + 1)]
    rest, given = total - bound - (number_of - 1), [1] * (number_of - 1)
    while rest > 0:
        free = [i for i in range(number_of - 1) if given[i] < bound]
        whole, remaining = sum([loads[i] for i in free]), rest
        for i in free:
            extra = min(bound - given[i], max(1, remaining * loads[i] // whole), rest)
            given[i] = given[i] + extra
            rest = rest - extra
    return np.array([bound] + given)


def uneven_parts(key, number_of, total, bound, slope):
    if number_of == 2:
        one = jax.random.randint(key, (), max(1, total - bound), min(bound, total - 1) + 1)
        return jnp.stack([one, total - one])
    tallies = jnp.asarray(split_up(number_of, total, bound, slope), jnp.int32)
    couples = (number_of - 1) // 2
    giver, receiver = tallies[1:1 + 2 * couples:2], tallies[2:2 + 2 * couples:2]
    slack = jnp.minimum(giver - 1, bound - receiver)
    moved = jax.random.randint(jax.random.fold_in(key, 1), (couples,), 0, 1 << 20) % (slack + 1)
    tallies = tallies.at[1:1 + 2 * couples:2].set(giver - moved).at[2:2 + 2 * couples:2].set(receiver + moved)
    return tallies[jax.random.permutation(jax.random.fold_in(key, 2), number_of)]


def routed_block(rng, own, number, rows, amount, top, reach, lean):
    sequence = jax.random.permutation(rng, amount)
    packed, common = portions_of(amount, rows * top, reach, lean, True), portions_of(amount, rows * top, reach, lean, False)
    places = jnp.arange(amount)

    def named(sizes, offset_by):
        used = int((sizes > 0).sum())
        fixed = max(1, used // 4)
        shifted = fixed + (places - fixed + offset_by * (used - fixed)) % max(1, amount - fixed)
        return jnp.zeros((amount,), jnp.int32).at[sequence[jnp.where(places < fixed, places, shifted)]].set(jnp.asarray(sizes, jnp.int32))

    sizes = jnp.where(number % 4 == 0, named(packed, number // 4), named(common, number - number // 4 - 1))
    mixed = jax.random.permutation(jax.random.fold_in(own, 3), amount)
    donor, sink = mixed[0:amount // 2 * 2:2], mixed[1:amount // 2 * 2:2]
    slack = jnp.minimum(sizes[donor] - 1, reach - sizes[sink]) // 2
    slack = jnp.where((donor == sequence[0]) | (sink == sequence[0]) | (sizes[sink] == 0), 0, jnp.maximum(slack, 0))
    shifted = jax.random.randint(jax.random.fold_in(own, 4), (amount // 2,), 0, 1 << 20) % (slack + 1)
    sizes = sizes.at[donor].add(-shifted).at[sink].add(shifted)
    labels = jnp.searchsorted(jnp.cumsum(sizes), jnp.arange(rows * top), side="right").astype(jnp.int32)
    grid = labels.reshape(top, rows).T
    grid = grid[jax.random.permutation(jax.random.fold_in(own, 1), rows)]
    offset_by = jax.random.randint(jax.random.fold_in(own, 2), (rows, 1), 0, top)
    return jnp.take_along_axis(grid, (jnp.arange(top)[None, :] + offset_by) % top, axis=1)


def portions_of(amount, total, most, skew, full):
    portions = [(1 << 20) // math.isqrt(grade ** skew) + 1 for grade in range(1, amount + 1)]
    largest = most if full else min(most, max(-(-total // amount), total * portions[0] // sum(portions)))
    least = 1 if total - largest >= amount - 1 else 0
    given, spare = [largest] + [least] * (amount - 1), total - largest - least * (amount - 1)
    while spare > 0:
        free = [i for i in range(1, amount) if given[i] < largest] or [i for i in range(1, amount) if given[i] < most]
        pool, budget = sum([portions[i] for i in free]), spare
        for i in free:
            extra = min(most - given[i], max(1, budget * portions[i] // pool), spare)
            given[i] = given[i] + extra
            spare = spare - extra
    return np.array(given)


def gaussian(key, extent, deviation, bound, shards=(), kind=jnp.bfloat16):
    entries = jax.random.normal(key, extent, jnp.float32) * deviation
    if len(shards) > 0:
        entries = shard_levels(key, extent, shards, -0.22, 0.18) * entries
    return jnp.clip(entries, min=-bound, max=bound).astype(kind)


def gaussian_with(key, extent, scale, limit, shards, heavy, held_as=jnp.bfloat16):
    array = scale * jax.random.normal(key, extent, jnp.float32)
    if shards:
        array = array * shard_levels(key, extent, shards, -0.22, 0.18)
    return jnp.clip(raised(array, jax.random.fold_in(key, 3), *heavy), -limit, limit).astype(held_as)


def setup_inputs(seed: int = 0) -> dict:
    streams_of = jax.random.split(jax.random.key(seed), 11)
    tokens = gaussian(streams_of[0], (BATCH, LEVELS, LAT, LON, D), 1.0, 6.0, ((0, 2), (2, 4), (3, 4)))
    norm_gain = jnp.clip(1.0 + 0.18 * jax.random.normal(streams_of[1], (D,), jnp.float32), 0.1, 1.9)
    w_qkv = draw_w_qkv(jax.random.fold_in(streams_of[10], 71), 0)
    w_out = gaussian(streams_of[3], (D, D), D ** -0.5, 0.1875)
    obs_vectors = gaussian(streams_of[4], (OBS, D), 1.0, 6.0, ((0, 32),))
    obs_lat_keys = jax.random.split(jax.random.fold_in(streams_of[5], 1), OBS // OBS_DEV)
    obs_lat_turns = jax.random.permutation(jax.random.fold_in(streams_of[5], 3), OBS // OBS_DEV)
    obs_lat = jax.vmap(lambda own, number: routed_block(jax.random.fold_in(streams_of[5], 2), own, number, OBS_DEV, N_LAT, 1, CAP, 2))(obs_lat_keys, obs_lat_turns).reshape((OBS, 1))
    obs_cell = touch_ends(jax.random.randint(streams_of[6], (OBS,), 0, TOK_DEV), jax.random.fold_in(streams_of[6], 1), 0, TOK_DEV - 1).astype(jnp.int32)
    obs_count = uneven_parts(streams_of[7], DEVICES, DEVICES * OBS_DEV * 3 // 4, OBS_DEV, 2).astype(jnp.int32)
    shift_offsets = draw_shift_offsets(jax.random.fold_in(streams_of[10], 71), 0)
    cotangent = gaussian_with(streams_of[9], (BATCH, LEVELS, LAT, LON, D), ALL_TOK ** -0.5, 0.09375, ((0, 2), (2, 4), (3, 4)), (3, 4, 4, 2.0))
    return {"tokens": tokens, "norm_gain": norm_gain, "w_qkv": w_qkv, "w_out": w_out, "obs_vectors": obs_vectors, "obs_lat": obs_lat, "obs_cell": obs_cell, "obs_count": obs_count, "shift_offsets": shift_offsets, "cotangent": cotangent}


def to_windows(field_in):
    levels_n, rows_n, cols_n, feat_width = field_in.shape
    blocks = field_in.reshape(levels_n, rows_n // WIN, WIN, cols_n // WIN, WIN, feat_width)
    return blocks.transpose(1, 3, 0, 2, 4, 5).reshape(-1, levels_n * WIN * WIN, feat_width)

def from_windows(windows, levels_n, rows_n, cols_n):
    feat_width = windows.shape[-1]
    blocks = windows.reshape(rows_n // WIN, cols_n // WIN, levels_n, WIN, WIN, feat_width)
    return blocks.transpose(2, 0, 3, 1, 4, 5).reshape(levels_n, rows_n, cols_n, feat_width)

def window_block(win_tokens, win_valid, norm_gain, w_qkv, w_out):
    n_win, n_tok, d_model = win_tokens.shape
    head_dim = d_model // HEADS
    as_float = win_tokens.astype(jnp.float32)
    average = lax.optimization_barrier(jnp.mean(as_float, axis=-1, keepdims=True))
    centred = as_float - average
    variance = lax.optimization_barrier(jnp.mean(centred * centred, axis=-1, keepdims=True))
    normed = (centred * lax.rsqrt(variance + 1e-05) * norm_gain).astype(jnp.bfloat16)
    projected = jnp.dot(normed.reshape(-1, d_model), w_qkv, preferred_element_type=jnp.float32).astype(jnp.bfloat16)
    projected = projected.reshape(n_win, n_tok, 3, HEADS, head_dim)
    queries = projected[:, :, 0].astype(jnp.float32)
    key_rows = projected[:, :, 1].astype(jnp.float32)
    values = projected[:, :, 2].astype(jnp.float32)
    scores = jnp.einsum('wqhd,wkhd->whqk', queries, key_rows) * head_dim ** (-0.5)
    scores = jnp.where(win_valid[:, None, None, :], scores, -1e+30)
    highest = lax.optimization_barrier(jnp.max(scores, axis=-1, keepdims=True))
    powers = jnp.exp(scores - highest)
    weights = (powers / lax.optimization_barrier(jnp.sum(powers, axis=-1, keepdims=True))).astype(jnp.bfloat16)
    context = jnp.einsum('whqk,wkhd->wqhd', weights.astype(jnp.float32), values).astype(jnp.bfloat16)
    context = context.reshape(n_win, n_tok, d_model)
    result = jnp.dot(context.reshape(-1, d_model), w_out, preferred_element_type=jnp.float32)
    return ((as_float + result.reshape(n_win, n_tok, d_model)).astype(jnp.bfloat16), context)

def reference(tokens, norm_gain, w_qkv, w_out, obs_vectors, obs_lat, obs_cell, obs_count, shift_offsets, cotangent):
    n_batch, levels, n_rows, n_cols, d_model = tokens.shape
    row_ids = jnp.arange(obs_vectors.shape[0], dtype=jnp.int32)
    device = row_ids // OBS_DEV
    within = row_ids % OBS_DEV
    is_live = within < obs_count[device]
    lon_index = device // (N_LAT * N_DP)
    sample = device % N_DP
    level_of = obs_cell // (LAT_DEV * LON_DEV)
    row_of = obs_lat[:, 0] * LAT_DEV + obs_cell // LON_DEV % LAT_DEV
    col_of = lon_index * LON_DEV + obs_cell % LON_DEV
    addend = jnp.where(is_live[:, None], obs_vectors.astype(jnp.float32), jnp.zeros((), jnp.float32))
    enriched = tokens.astype(jnp.float32).at[sample, level_of, row_of, col_of].add(addend).astype(jnp.bfloat16)
    lat_blocks = n_rows // WIN

    def roll_sample(pair):
        grid_in, offset_pair = pair
        turned = jnp.roll(grid_in, -offset_pair[1], axis=2)
        padded = jnp.concatenate([turned, jnp.zeros((levels, WIN, n_cols, d_model), turned.dtype)], axis=1)
        anchor = jnp.zeros((), jnp.int32)
        return lax.dynamic_slice(padded, (anchor, offset_pair[0].astype(jnp.int32), anchor, anchor), grid_in.shape)
    rolled = lax.map(roll_sample, (enriched, shift_offsets))

    def advance(gradient, position):
        sample_at = position // lat_blocks
        start_row = (position % lat_blocks * WIN).astype(jnp.int32)
        strip_in = lax.dynamic_slice_in_dim(rolled[sample_at], start_row, WIN, 1)
        cot_strip = lax.dynamic_slice_in_dim(cotangent[sample_at], start_row, WIN, 1)
        global_rows = start_row + jnp.arange(WIN, dtype=jnp.int32) + shift_offsets[sample_at, 0]
        is_valid = jnp.broadcast_to((global_rows < n_rows)[None, :, None, None], (levels, WIN, n_cols, 1))
        mixed, context = window_block(to_windows(strip_in), to_windows(is_valid)[..., 0], norm_gain, w_qkv, w_out)
        cot_rows = to_windows(cot_strip).reshape(-1, d_model)
        gradient = gradient + jnp.dot(cot_rows.T, context.reshape(-1, d_model), preferred_element_type=jnp.float32)
        return (gradient, from_windows(mixed, levels, WIN, n_cols))
    gradient, strips = lax.scan(advance, jnp.zeros((d_model, d_model), jnp.float32), jnp.arange(n_batch * lat_blocks, dtype=jnp.int32))
    block_out = strips.reshape(n_batch, lat_blocks, levels, WIN, n_cols, d_model).transpose(0, 2, 1, 3, 4, 5).reshape(tokens.shape)
    return (block_out, gradient)
```

```python
import functools

import jax
import jax.numpy as jnp
from jax import lax
from jax.experimental import pallas as pl
from jax.experimental.pallas import tpu as pltpu
from jax.sharding import PartitionSpec as P

HEADS = 16
WIN = 8
BF16 = jnp.bfloat16
F32 = jnp.float32
LANES = 128
VMEM_LIMIT = 48 * 1024 * 1024


def from_behind(array, axis, by):
    devices = lax.axis_size(axis)
    pairs = [(i, i + by) for i in range(devices) if 0 <= i + by < devices]
    return lax.ppermute(array, axis, pairs)


def shifted(array, axis, by):
    devices = lax.axis_size(axis)
    return lax.ppermute(array, axis, [(i, (i + by) % devices) for i in range(devices)])


def swapped(array, axis, bit):
    devices = lax.axis_size(axis)
    return lax.ppermute(array, axis, [(i, i ^ bit) for i in range(devices)])


def to_windows(field_in):
    levels_n, rows_n, cols_n, feat_width = field_in.shape
    blocks = field_in.reshape(levels_n, rows_n // WIN, WIN, cols_n // WIN, WIN, feat_width)
    return blocks.transpose(1, 3, 0, 2, 4, 5).reshape(-1, levels_n * WIN * WIN, feat_width)


def from_windows(windows, levels_n, rows_n, cols_n):
    feat_width = windows.shape[-1]
    blocks = windows.reshape(rows_n // WIN, cols_n // WIN, levels_n, WIN, WIN, feat_width)
    return blocks.transpose(2, 0, 3, 1, 4, 5).reshape(levels_n, rows_n, cols_n, feat_width)


def window_block(win_tokens, win_valid, norm_gain, w_qkv, w_out):
    n_win, n_tok, d_model = win_tokens.shape
    head_dim = d_model // HEADS
    as_float = win_tokens.astype(F32)
    average = jnp.mean(as_float, axis=-1, keepdims=True)
    centred = as_float - average
    variance = jnp.mean(centred * centred, axis=-1, keepdims=True)
    normed = (centred * lax.rsqrt(variance + 1e-05) * norm_gain).astype(BF16)
    projected = jnp.dot(
        normed.reshape(-1, d_model), w_qkv, preferred_element_type=F32
    ).astype(BF16)
    projected = projected.reshape(n_win, n_tok, 3, HEADS, head_dim)
    queries = projected[:, :, 0]
    key_rows = projected[:, :, 1]
    values = projected[:, :, 2]
    scores = jnp.einsum(
        "wqhd,wkhd->whqk", queries, key_rows, preferred_element_type=F32
    ) * head_dim ** (-0.5)
    scores = jnp.where(win_valid[:, None, None, :], scores, -1e30)
    highest = jnp.max(scores, axis=-1, keepdims=True)
    powers = jnp.exp(scores - highest)
    weights = (powers / jnp.sum(powers, axis=-1, keepdims=True)).astype(BF16)
    context = jnp.einsum(
        "whqk,wkhd->wqhd", weights, values, preferred_element_type=F32
    ).astype(BF16)
    context = context.reshape(n_win, n_tok, d_model)
    result = jnp.dot(context.reshape(-1, d_model), w_out, preferred_element_type=F32)
    return ((as_float + result.reshape(n_win, n_tok, d_model)).astype(BF16), context)


def general_program(
    tokens, norm_gain, w_qkv, w_out, obs_vectors, obs_lat, obs_cell, obs_count, shift_offsets, cotangent
):
    n_batch, levels, lat_dev, lon_dev, d_model = tokens.shape
    n_lat = lax.axis_size("lat")
    obs_rows = obs_vectors.shape[0]
    capacity = obs_rows * 3 // (2 * n_lat)
    n_slots = n_lat * capacity
    destination = obs_lat[:, 0]
    one_hot = (destination[:, None] == jnp.arange(n_lat, dtype=jnp.int32)[None, :]).astype(jnp.int32)
    earlier = jnp.cumsum(one_hot, axis=0) - one_hot
    rank_in = jnp.sum(earlier * one_hot, axis=1)
    slot_of = destination * capacity + rank_in
    is_live = jnp.arange(obs_rows, dtype=jnp.int32) < obs_count[0]
    cell_tag = jnp.where(is_live, obs_cell, -1)
    chooser = slot_of[None, :] == jnp.arange(n_slots, dtype=jnp.int32)[:, None]
    sent_rows = (
        jnp.dot(chooser.astype(BF16), obs_vectors, preferred_element_type=F32)
        .astype(BF16)
        .reshape(n_lat, capacity, d_model)
    )
    sent_tags = (jnp.sum(chooser.astype(jnp.int32) * (cell_tag[None, :] + 1), axis=1) - 1).reshape(
        n_lat, capacity
    )
    got_rows, got_tags = (
        lax.all_to_all(sent_rows, "lat", split_axis=0, concat_axis=0, tiled=True),
        lax.all_to_all(sent_tags, "lat", split_axis=0, concat_axis=0, tiled=True),
    )
    flat_tokens = tokens.reshape(-1, d_model)
    placer = (
        got_tags.reshape(-1)[None, :] == jnp.arange(flat_tokens.shape[0], dtype=jnp.int32)[:, None]
    ).astype(BF16)
    added = jnp.dot(placer, got_rows.reshape(-1, d_model), preferred_element_type=F32)
    enriched = (flat_tokens.astype(F32) + added).astype(BF16).reshape(tokens.shape)
    margin = WIN - 1
    north_part = from_behind(enriched[:, :, :margin], "lat", -1)
    heightened = jnp.concatenate([enriched, north_part], axis=2)
    east_cols = shifted(heightened[:, :, :, :margin], "lon", -1)
    extended = jnp.concatenate([heightened, east_cols], axis=3)
    lat_shift = shift_offsets[0, 0]
    lon_shift = shift_offsets[0, 1]
    anchor = jnp.zeros((), jnp.int32)
    region = lax.dynamic_slice(
        extended, (anchor, anchor, lat_shift, lon_shift, anchor), tokens.shape
    )[0]
    source_rows = lax.axis_index("lat") * lat_dev + lat_shift + jnp.arange(lat_dev, dtype=jnp.int32)
    is_valid = jnp.broadcast_to(
        (source_rows < lat_dev * n_lat)[None, :, None, None], (levels, lat_dev, lon_dev, 1)
    )
    mixed, context = window_block(
        to_windows(region), to_windows(is_valid)[..., 0], norm_gain, w_qkv, w_out
    )
    block_out = from_windows(mixed, levels, lat_dev, lon_dev)[None]
    cot_rows = to_windows(cotangent[0]).reshape(-1, d_model)
    context_rows = context.reshape(-1, d_model)
    contract = (((0,), (0,)), ((), ()))
    partial_rows = lax.psum_scatter(
        lax.dot_general(cot_rows, context_rows, contract, preferred_element_type=F32),
        "lon",
        scatter_dimension=0,
        tiled=True,
    )
    gradient = lax.psum_scatter(partial_rows, ("lat", "dp"), scatter_dimension=1, tiled=True)
    return (block_out, gradient)


def call(body, out_shape, args, specs, name, scratch=(), flops=0, moved=0):
    return pl.pallas_call(
        body,
        out_shape=out_shape,
        in_specs=specs,
        out_specs=jax.tree.map(lambda _: pl.BlockSpec(memory_space=pltpu.VMEM), out_shape),
        scratch_shapes=list(scratch),
        compiler_params=pltpu.CompilerParams(vmem_limit_bytes=VMEM_LIMIT),
        cost_estimate=pl.CostEstimate(flops=flops, bytes_accessed=moved, transcendentals=0),
        name=name,
    )(*args)


VMEM_SPEC = pl.BlockSpec(memory_space=pltpu.VMEM)
SMEM_SPEC = pl.BlockSpec(memory_space=pltpu.SMEM)


def iota(shape, dim):
    return lax.broadcasted_iota(jnp.int32, shape, dim)


def over_rows(lhs, rhs):
    return lax.dot_general(lhs, rhs, (((0,), (0,)), ((), ())), preferred_element_type=F32)


def matmul(lhs, rhs):
    return jnp.dot(lhs, rhs, preferred_element_type=F32)


def route_body(n_lat, cap, slots, count_ref, lat_ref, cell_ref, vec_ref, *out_refs):
    rows = vec_ref.shape[0]
    here = lax.axis_index("lat")
    lane = iota((rows, LANES), 1)
    lat = lat_ref[...]
    named = (lat == lane).astype(BF16)
    below = (iota((rows, rows), 0) > iota((rows, rows), 1)).astype(BF16)
    rank = jnp.sum(matmul(below, named) * named.astype(F32), axis=1, keepdims=True)
    turn = jnp.where(lat < here, lat - here + n_lat, lat - here)
    base = turn * slots
    chooser = (base + rank.astype(jnp.int32) == lane).astype(BF16)
    live = iota((1, rows), 1) < count_ref[0]
    tag_row = jnp.where(live, cell_ref[...] + 1, 0).astype(F32)
    same = iota((rows, rows), 0) == iota((rows, rows), 1)
    tag = jnp.sum(jnp.where(same, tag_row, 0.0), axis=1, keepdims=True)
    tag_at = jnp.where(lane == base + cap, tag, 0.0).astype(BF16)
    picked = over_rows(chooser, vec_ref[...])
    tags = over_rows(tag_at, chooser)
    for k, out_ref in enumerate(out_refs):
        piece = slice(k * slots, (k + 1) * slots)
        out_ref[:, :LANES] = (picked[piece, :LANES] + tags[piece]).astype(BF16)
        out_ref[:, LANES:] = picked[piece, LANES:].astype(BF16)


def enrich_body(n_lat, cap, tok_ref, *refs):
    parts, (own_ref, north_ref, east_ref) = refs[:n_lat], refs[n_lat:]
    _, levels, rows, cols, width = tok_ref.shape
    tags = parts[0][cap : cap + 1, :LANES].astype(F32)
    for part in parts[1:]:
        tags = tags + part[cap : cap + 1, :LANES].astype(F32)
    n_tok = levels * rows * cols
    place = (tags.astype(jnp.int32) == iota((n_tok, LANES), 0) + 1).astype(BF16)
    added = matmul(place, jnp.concatenate([part[...] for part in parts], axis=0))
    total = tok_ref[...].reshape(n_tok, width).astype(F32) + added
    own_ref[...] = total.astype(BF16)
    margin = (rows - 1) * cols
    for level in range(levels):
        start = level * rows * cols
        north_ref[level * margin : (level + 1) * margin] = total[start : start + margin].astype(BF16)
    east_ref[...] = (
        total.reshape(levels * rows, cols, width)[:, :WIN].reshape(-1, width).astype(BF16)
    )


def corner_body(north_ref, out_ref):
    rows, width = north_ref.shape
    grid = north_ref[...].astype(F32).reshape(rows // (2 * WIN), 2 * WIN, width)
    out_ref[...] = grid[:, :WIN].reshape(-1, width).astype(BF16)


def window_body(which, n_lat, n_dp, n_src, shift_ref, *refs):
    sources = refs[:n_src]
    gain_ref, wqkv_ref, region_ref, ctx_ref, send_ref, keep_ref, qkv_ref = refs[n_src:]
    width = gain_ref.shape[1]
    n_tok = region_ref.shape[0]
    half = width // n_dp
    d_blk = half // n_lat
    lat_shift, lon_shift = shift_ref[0, 0], shift_ref[0, 1]
    row = iota((n_tok, 1), 0)
    level = row // (WIN * WIN)
    at_lat = row // WIN % WIN + lat_shift
    at_lon = row % WIN + which * WIN + lon_shift
    cols = 2 * WIN
    inside, over = at_lat < WIN, at_lat >= WIN
    near, far = at_lon < cols, at_lon >= cols
    margin = WIN - 1
    wanted = [
        (inside & near, (level * WIN + at_lat) * cols + at_lon),
        (over & near, (level * margin + at_lat - WIN) * cols + at_lon),
        (inside & far, (level * WIN + at_lat) * WIN + at_lon - cols),
        (over & far, (level * margin + at_lat - WIN) * WIN + at_lon - cols),
    ]
    region = None
    for source, (here, index) in zip(sources, wanted):
        index = jnp.where(here, index, -1)
        pick = (index == iota((n_tok, source.shape[0]), 1)).astype(BF16)
        part = matmul(pick, source[...])
        region = part if region is None else region + part
    region_ref[...] = region.astype(BF16)
    centred = region - jnp.mean(region, axis=-1, keepdims=True)
    variance = jnp.mean(centred * centred, axis=-1, keepdims=True)
    normed = (centred * lax.rsqrt(variance + 1e-05) * gain_ref[...]).astype(BF16)
    for third in range(3):
        piece = slice(third * width, (third + 1) * width)
        qkv_ref[:, piece] = matmul(normed, wqkv_ref[:, piece]).astype(BF16)
    key = iota((1, n_tok), 1)
    n_rows = WIN * n_lat
    valid = lax.axis_index("lat") * WIN + key // WIN % WIN + lat_shift < n_rows
    first = iota((n_tok, d_blk), 1) < d_blk // 2
    scale = (d_blk // 2) ** (-0.5)
    ones = jnp.ones((n_tok, d_blk), BF16)
    lat_at, dp_at = lax.axis_index("lat"), lax.axis_index("dp")
    for part, out_ref in ((1 - dp_at, send_ref), (dp_at, keep_ref)):
        for k in range(n_lat):
            lat = lat_at + k
            lat = jnp.where(lat >= n_lat, lat - n_lat, lat)
            at = pl.multiple_of((lat * n_dp + part) * d_blk, d_blk)
            query = qkv_ref[:, pl.ds(at, d_blk)].astype(F32) * scale
            both = jnp.concatenate(
                [jnp.where(first, query, 0.0), jnp.where(first, 0.0, query)], axis=0
            ).astype(BF16)
            keys = qkv_ref[:, pl.ds(width + at, d_blk)]
            scores = lax.dot_general(
                both, keys, (((1,), (1,)), ((), ())), preferred_element_type=F32
            )
            scores = jnp.where(valid, scores, -1e30)
            powers = jnp.exp(scores - jnp.max(scores, axis=-1, keepdims=True)).astype(BF16)
            values = jnp.concatenate([qkv_ref[:, pl.ds(2 * width + at, d_blk)], ones], axis=1)
            mixed = matmul(powers, values)
            mixed = mixed[:, :d_blk] / mixed[:, d_blk:]
            context = jnp.where(first, mixed[:n_tok], mixed[n_tok:]).astype(BF16)
            out_ref[:, k * d_blk : (k + 1) * d_blk] = context
            ctx_ref[:, pl.ds(at, d_blk)] = context


def turn_body(n_lon, cot_ref, other_ref, out_ref, flat_ref):
    _, levels, rows, cols, width = cot_ref.shape
    e_blk = width // n_lon
    n_tok = levels * rows * WIN
    here = lax.axis_index("lon")
    at = 0
    for ref in (cot_ref, other_ref):
        grid = ref[...].astype(F32).reshape(levels * rows, cols, width)
        for which in range(cols // WIN):
            flat_ref[...] = grid[:, which * WIN : (which + 1) * WIN].reshape(n_tok, width)
            for place, block in enumerate(reversed_order(n_lon)):
                lon = here ^ block
                piece = flat_ref[:, pl.ds(pl.multiple_of(lon * e_blk, e_blk), e_blk)]
                out_ref[place, :, at : at + n_tok] = piece.T.astype(BF16)
            at += n_tok


def reversed_order(count):
    bits = count.bit_length() - 1
    return [int(format(i, f"0{bits}b")[::-1], 2) if bits else 0 for i in range(count)]


def project_body(reg0_ref, reg1_ref, ctx0_ref, ctx1_ref, wout_ref, out_ref):
    _, levels, rows, cols, width = out_ref.shape
    halves = []
    for reg_ref, ctx_ref in ((reg0_ref, ctx0_ref), (reg1_ref, ctx1_ref)):
        mixed = reg_ref[...].astype(F32) + matmul(ctx_ref[...], wout_ref[...])
        halves.append(mixed.reshape(levels * rows, WIN, width))
    whole = jnp.concatenate(halves, axis=1).astype(BF16)
    out_ref[...] = whole.reshape(out_ref.shape)


def gradient_body(cot_ref, *refs):
    ctx_refs, (keep_ref, send_ref) = refs[:-2], refs[-2:]
    context = jnp.concatenate([ref[...] for ref in ctx_refs], axis=0)
    count = cot_ref.shape[0] // 2
    for place in range(count):
        keep_ref[place] = matmul(cot_ref[place], context)
        send_ref[place] = matmul(cot_ref[count + place], context).astype(BF16)


def fast_program(
    tokens, norm_gain, w_qkv, w_out, obs_vectors, obs_lat, obs_cell, obs_count, shift_offsets, cotangent
):
    _, levels, lat_dev, lon_dev, d_model = tokens.shape
    n_lat, n_lon, n_dp = (lax.axis_size(axis) for axis in ("lat", "lon", "dp"))
    obs_rows = obs_vectors.shape[0]
    cap = obs_rows * 3 // (2 * n_lat)
    slots = LANES // n_lat
    shape = jax.ShapeDtypeStruct
    n_tok = levels * WIN * WIN
    margin = WIN - 1
    half = d_model // n_dp
    e_blk = d_model // n_lon
    d_blk = half // n_lat

    payload = call(
        functools.partial(route_body, n_lat, cap, slots),
        [shape((slots, d_model), BF16)] * n_lat,
        (obs_count, obs_lat, obs_cell.reshape(1, -1), obs_vectors),
        [SMEM_SPEC, VMEM_SPEC, VMEM_SPEC, VMEM_SPEC],
        "route",
    )
    arrived = [payload[0]] + [shifted(payload[k], "lat", k) for k in range(1, n_lat)]
    own, north, east = call(
        functools.partial(enrich_body, n_lat, cap),
        [
            shape((levels * lat_dev * lon_dev, d_model), BF16),
            shape((levels * margin * lon_dev, d_model), BF16),
            shape((levels * lat_dev * WIN, d_model), BF16),
        ],
        (tokens, *arrived),
        [VMEM_SPEC] * (1 + n_lat),
        "enrich",
    )
    north = from_behind(north, "lat", -1)
    east = shifted(east, "lon", -1)
    cot_other = swapped(cotangent, "dp", 1)
    corner = call(
        corner_body,
        shape((levels * margin * WIN, d_model), BF16),
        (north,),
        [VMEM_SPEC],
        "corner",
    )
    corner = shifted(corner, "lon", -1)
    cot_turned = call(
        functools.partial(turn_body, n_lon),
        shape((n_lon, e_blk, n_dp * lon_dev // WIN * n_tok), BF16),
        (cotangent, cot_other),
        [VMEM_SPEC] * 2,
        "turn",
        [pltpu.VMEM((n_tok, d_model), F32)],
    )
    gain = norm_gain.reshape(1, -1)
    windows = []
    for which, sources in enumerate(((own, north), (own, north, east, corner))):
        windows.append(
            call(
                functools.partial(window_body, which, n_lat, n_dp, len(sources)),
                [
                    shape((n_tok, d_model), BF16),
                    shape((n_tok, d_model), BF16),
                    shape((n_tok, half), BF16),
                    shape((n_tok, half), BF16),
                ],
                (shift_offsets, *sources, gain, w_qkv),
                [SMEM_SPEC] + [VMEM_SPEC] * (len(sources) + 2),
                f"window{which}",
                [pltpu.VMEM((n_tok, 3 * d_model), BF16)],
                flops=2 * n_tok * d_model * 3 * d_model,
            )
        )
    (region0, ctx0, send0, keep0), (region1, ctx1, send1, keep1) = windows
    got0 = swapped(send0, "dp", 1)
    got1 = swapped(send1, "dp", 1)
    block_out = call(
        project_body,
        shape(tokens.shape, BF16),
        (region0, region1, ctx0, ctx1, w_out),
        [VMEM_SPEC] * 5,
        "project",
        flops=4 * n_tok * d_model * d_model,
    )
    kept, sent = call(
        gradient_body,
        [shape((n_lon // 2, e_blk, half), F32), shape((n_lon // 2, e_blk, half), BF16)],
        (cot_turned, keep0, keep1, got0, got1),
        [VMEM_SPEC] * 5,
        "gradient",
        flops=4 * n_tok * d_model * d_model,
    )
    bit = 1
    while True:
        total = kept + swapped(sent, "lon", bit).astype(F32)
        bit *= 2
        if bit == n_lon:
            break
        middle = total.shape[0] // 2
        kept, sent = total[:middle], total[middle:].astype(BF16)
    total = total[0]
    blocks = [total[:, k * d_blk : (k + 1) * d_blk] for k in range(n_lat)]
    gradient = blocks[0]
    for k in range(1, n_lat):
        gradient = gradient + shifted(blocks[k].astype(BF16), "lat", k).astype(F32)
    return (block_out, gradient)


def on_device(tokens, norm_gain, w_qkv, w_out, obs_vectors, *rest):
    _, _, lat_dev, lon_dev, d_model = tokens.shape
    n_lat, n_lon, n_dp = (lax.axis_size(axis) for axis in ("lat", "lon", "dp"))
    cap = obs_vectors.shape[0] * 3 // (2 * n_lat)
    fits = (
        n_dp == 2
        and n_lon > 1
        and n_lon & (n_lon - 1) == 0
        and LANES % n_lat == 0
        and cap < LANES // n_lat
        and lat_dev == WIN
        and lon_dev == 2 * WIN
        and d_model // n_lon % LANES == 0
        and d_model // (n_lat * n_dp) == LANES
        and d_model // HEADS * 2 == LANES
    )
    program = fast_program if fits else general_program
    return program(tokens, norm_gain, w_qkv, w_out, obs_vectors, *rest)


def solution(mesh):
    placed = (
        P("dp", None, "lat", "lon", None),
        P(),
        P(),
        P(),
        P(("lon", "lat", "dp"), None),
        P(("lon", "lat", "dp"), None),
        P(("lon", "lat", "dp")),
        P(("lon", "lat", "dp")),
        P("dp", None),
        P("dp", None, "lat", "lon", None),
    )
    return jax.shard_map(
        on_device,
        mesh=mesh,
        in_specs=placed,
        out_specs=(P("dp", None, "lat", "lon", None), P("lon", ("lat", "dp"))),
        check_vma=False,
    )
```

```python
import functools

import jax
import jax.numpy as jnp
from jax import lax
from jax.experimental import pallas as pl
from jax.experimental.pallas import tpu as pltpu
from jax.sharding import PartitionSpec as P

HEADS = 16
WIN = 8
BF16 = jnp.bfloat16
F32 = jnp.float32
LANES = 128
TILE = 16
VMEM_LIMIT = 24 * 1024 * 1024
SLOW = 10**10


def from_behind(array, axis, by):
    devices = lax.axis_size(axis)
    pairs = [(i, i + by) for i in range(devices) if 0 <= i + by < devices]
    return lax.ppermute(array, axis, pairs)


def shifted(array, axis, by):
    devices = lax.axis_size(axis)
    return lax.ppermute(array, axis, [(i, (i + by) % devices) for i in range(devices)])


def swapped(array, axis, bit):
    devices = lax.axis_size(axis)
    return lax.ppermute(array, axis, [(i, i ^ bit) for i in range(devices)])


def to_windows(field_in):
    levels_n, rows_n, cols_n, feat_width = field_in.shape
    blocks = field_in.reshape(levels_n, rows_n // WIN, WIN, cols_n // WIN, WIN, feat_width)
    return blocks.transpose(1, 3, 0, 2, 4, 5).reshape(-1, levels_n * WIN * WIN, feat_width)


def from_windows(windows, levels_n, rows_n, cols_n):
    feat_width = windows.shape[-1]
    blocks = windows.reshape(rows_n // WIN, cols_n // WIN, levels_n, WIN, WIN, feat_width)
    return blocks.transpose(2, 0, 3, 1, 4, 5).reshape(levels_n, rows_n, cols_n, feat_width)


def window_block(win_tokens, win_valid, norm_gain, w_qkv, w_out):
    n_win, n_tok, d_model = win_tokens.shape
    head_dim = d_model // HEADS
    as_float = win_tokens.astype(F32)
    average = jnp.mean(as_float, axis=-1, keepdims=True)
    centred = as_float - average
    variance = jnp.mean(centred * centred, axis=-1, keepdims=True)
    normed = (centred * lax.rsqrt(variance + 1e-05) * norm_gain).astype(BF16)
    projected = jnp.dot(
        normed.reshape(-1, d_model), w_qkv, preferred_element_type=F32
    ).astype(BF16)
    projected = projected.reshape(n_win, n_tok, 3, HEADS, head_dim)
    queries = projected[:, :, 0]
    key_rows = projected[:, :, 1]
    values = projected[:, :, 2]
    scores = jnp.einsum(
        "wqhd,wkhd->whqk", queries, key_rows, preferred_element_type=F32
    ) * head_dim ** (-0.5)
    scores = jnp.where(win_valid[:, None, None, :], scores, -1e30)
    highest = jnp.max(scores, axis=-1, keepdims=True)
    powers = jnp.exp(scores - highest)
    weights = (powers / jnp.sum(powers, axis=-1, keepdims=True)).astype(BF16)
    context = jnp.einsum(
        "whqk,wkhd->wqhd", weights, values, preferred_element_type=F32
    ).astype(BF16)
    context = context.reshape(n_win, n_tok, d_model)
    result = jnp.dot(context.reshape(-1, d_model), w_out, preferred_element_type=F32)
    return ((as_float + result.reshape(n_win, n_tok, d_model)).astype(BF16), context)


def general_program(
    tokens, norm_gain, w_qkv, w_out, obs_vectors, obs_lat, obs_cell, obs_count, shift_offsets, cotangent
):
    n_batch, levels, lat_dev, lon_dev, d_model = tokens.shape
    n_lat = lax.axis_size("lat")
    obs_rows = obs_vectors.shape[0]
    capacity = obs_rows * 3 // (2 * n_lat)
    n_slots = n_lat * capacity
    destination = obs_lat[:, 0]
    one_hot = (destination[:, None] == jnp.arange(n_lat, dtype=jnp.int32)[None, :]).astype(jnp.int32)
    earlier = jnp.cumsum(one_hot, axis=0) - one_hot
    rank_in = jnp.sum(earlier * one_hot, axis=1)
    slot_of = destination * capacity + rank_in
    is_live = jnp.arange(obs_rows, dtype=jnp.int32) < obs_count[0]
    cell_tag = jnp.where(is_live, obs_cell, -1)
    chooser = slot_of[None, :] == jnp.arange(n_slots, dtype=jnp.int32)[:, None]
    sent_rows = (
        jnp.dot(chooser.astype(BF16), obs_vectors, preferred_element_type=F32)
        .astype(BF16)
        .reshape(n_lat, capacity, d_model)
    )
    sent_tags = (jnp.sum(chooser.astype(jnp.int32) * (cell_tag[None, :] + 1), axis=1) - 1).reshape(
        n_lat, capacity
    )
    got_rows, got_tags = (
        lax.all_to_all(sent_rows, "lat", split_axis=0, concat_axis=0, tiled=True),
        lax.all_to_all(sent_tags, "lat", split_axis=0, concat_axis=0, tiled=True),
    )
    flat_tokens = tokens.reshape(-1, d_model)
    placer = (
        got_tags.reshape(-1)[None, :] == jnp.arange(flat_tokens.shape[0], dtype=jnp.int32)[:, None]
    ).astype(BF16)
    added = jnp.dot(placer, got_rows.reshape(-1, d_model), preferred_element_type=F32)
    enriched = (flat_tokens.astype(F32) + added).astype(BF16).reshape(tokens.shape)
    margin = WIN - 1
    north_part = from_behind(enriched[:, :, :margin], "lat", -1)
    heightened = jnp.concatenate([enriched, north_part], axis=2)
    east_cols = shifted(heightened[:, :, :, :margin], "lon", -1)
    extended = jnp.concatenate([heightened, east_cols], axis=3)
    lat_shift = shift_offsets[0, 0]
    lon_shift = shift_offsets[0, 1]
    anchor = jnp.zeros((), jnp.int32)
    region = lax.dynamic_slice(
        extended, (anchor, anchor, lat_shift, lon_shift, anchor), tokens.shape
    )[0]
    source_rows = lax.axis_index("lat") * lat_dev + lat_shift + jnp.arange(lat_dev, dtype=jnp.int32)
    is_valid = jnp.broadcast_to(
        (source_rows < lat_dev * n_lat)[None, :, None, None], (levels, lat_dev, lon_dev, 1)
    )
    mixed, context = window_block(
        to_windows(region), to_windows(is_valid)[..., 0], norm_gain, w_qkv, w_out
    )
    block_out = from_windows(mixed, levels, lat_dev, lon_dev)[None]
    cot_rows = to_windows(cotangent[0]).reshape(-1, d_model)
    context_rows = context.reshape(-1, d_model)
    contract = (((0,), (0,)), ((), ()))
    partial_rows = lax.psum_scatter(
        lax.dot_general(cot_rows, context_rows, contract, preferred_element_type=F32),
        "lon",
        scatter_dimension=0,
        tiled=True,
    )
    gradient = lax.psum_scatter(partial_rows, ("lat", "dp"), scatter_dimension=1, tiled=True)
    return (block_out, gradient)


def call(body, out_shape, args, specs, name, scratch=(), flops=1, moved=1):
    return pl.pallas_call(
        body,
        out_shape=out_shape,
        in_specs=specs,
        out_specs=jax.tree.map(lambda _: pl.BlockSpec(memory_space=pltpu.VMEM), out_shape),
        scratch_shapes=list(scratch),
        compiler_params=pltpu.CompilerParams(vmem_limit_bytes=VMEM_LIMIT),
        cost_estimate=pl.CostEstimate(flops=flops, bytes_accessed=moved, transcendentals=0),
        name=name,
    )(*args)


VMEM_SPEC = pl.BlockSpec(memory_space=pltpu.VMEM)
SMEM_SPEC = pl.BlockSpec(memory_space=pltpu.SMEM)
ANY_SPEC = pl.BlockSpec(memory_space=pl.ANY)


def iota(shape, dim):
    return lax.broadcasted_iota(jnp.int32, shape, dim)


def over_rows(lhs, rhs):
    return lax.dot_general(lhs, rhs, (((0,), (0,)), ((), ())), preferred_element_type=F32)


def matmul(lhs, rhs):
    return jnp.dot(lhs, rhs, preferred_element_type=F32)


def copy_all(pairs, sems):
    copies = [pltpu.make_async_copy(src, dst, sems.at[i]) for i, (src, dst) in enumerate(pairs)]
    for copy in copies:
        copy.start()
    return copies


def route_body(n_lat, count_ref, cell_hbm, lat_hbm, vec_hbm, *refs):
    out_refs, (cell_ref, lat_ref, vec_ref, sems) = refs[:n_lat], refs[n_lat:]
    copies = copy_all([(cell_hbm, cell_ref), (lat_hbm, lat_ref), (vec_hbm, vec_ref)], sems)
    rows = vec_ref.shape[0]
    here = lax.axis_index("lat")
    lane = iota((rows, LANES), 1)
    below = (iota((rows, rows), 0) > iota((rows, rows), 1)).astype(BF16)
    same = iota((rows, rows), 0) == iota((rows, rows), 1)
    copies[0].wait()
    copies[1].wait()
    tag = jnp.where(iota((1, rows), 1) < count_ref[0], cell_ref[...] + 1, 0)
    tag, lat = (
        jnp.sum(jnp.where(same, field.astype(F32), 0.0), axis=1, keepdims=True)
        for field in (tag, lat_ref[...])
    )
    lat = lat.astype(jnp.int32)
    named = (lat == lane).astype(BF16)
    rank = jnp.sum(matmul(below, named) * named.astype(F32), axis=1, keepdims=True)
    rank = rank.astype(jnp.int32)
    base = jnp.where(lat < here, lat - here + n_lat, lat - here) * TILE
    late = rank >= TILE
    choosers = [
        (jnp.where(chosen, base + rank - back, -1) == lane).astype(BF16)
        for chosen, back in ((rank < TILE, 0), (late, TILE), (late, TILE // 2))
    ]
    tags = sum(
        over_rows(jnp.where(lane == base + i, tag, 0.0).astype(BF16), chooser)
        for i, chooser in enumerate(choosers)
    )
    copies[2].wait()
    width = vec_ref.shape[1]
    picked = over_rows(choosers[0], vec_ref[...])
    extra = over_rows(choosers[1], vec_ref[:, : width // 2])
    extra = extra + over_rows(choosers[2], vec_ref[:, width // 2 :])
    for k, out_ref in enumerate(out_refs):
        piece = slice(k * TILE, (k + 1) * TILE)
        out_ref[:, :width] = picked[piece].astype(BF16)
        out_ref[:, width : width + width // 2] = extra[piece].astype(BF16)
        out_ref[:, width + width // 2 :] = tags[piece].astype(BF16)


def load_body(*refs):
    count = len(refs) // 2
    for copy in copy_all(list(zip(refs[:count], refs[count:-1])), refs[-1]):
        copy.wait()


def load(arrays, name):
    return call(
        load_body,
        [jax.ShapeDtypeStruct(array.shape, array.dtype) for array in arrays],
        tuple(in_hbm(array) for array in arrays),
        [ANY_SPEC] * len(arrays),
        name,
        [pltpu.SemaphoreType.DMA((len(arrays),))],
    )


def stage_body(sizes, shift_ref, tok_hbm, tok_ref, pick_ref, sem):
    copy = pltpu.make_async_copy(tok_hbm, tok_ref, sem)
    copy.start()
    lat_shift, lon_shift = shift_ref[:, :1], shift_ref[:, 1:]
    n_rows, n_cols = pick_ref.shape
    n_tok = n_rows // 2
    row = iota((n_rows, 1), 0)
    level = row // (WIN * WIN) % (n_tok // (WIN * WIN))
    at_lat = row // WIN % WIN + lat_shift
    at_lon = row % WIN + row // n_tok * WIN + lon_shift
    cols, margin = 2 * WIN, WIN - 1
    starts = [sum(sizes[:i]) for i in range(len(sizes))]
    inside = (level * WIN + at_lat) * cols + at_lon
    north = (level * margin + at_lat - WIN) * WIN + at_lon % WIN
    east = (level * WIN + at_lat) * WIN + at_lon - cols
    index = jnp.where(
        at_lat < WIN,
        jnp.where(at_lon < cols, inside, east + starts[3]),
        north + jnp.where(at_lon < WIN, starts[1], jnp.where(at_lon < cols, starts[2], starts[4])),
    )
    pick_ref[...] = (index == iota((n_rows, n_cols), 1)).astype(BF16)
    copy.wait()


def enrich_body(n_lat, tok_ref, *refs):
    parts, (own_ref, north0_ref, north1_ref, east_ref) = refs[:n_lat], refs[n_lat:]
    _, levels, rows, cols, width = tok_ref.shape
    n_tok = levels * rows * cols
    half = width // 2
    tags = sum(part[:, width + half :].astype(F32) for part in parts).astype(jnp.int32)
    row = iota((n_tok, LANES), 0) + 1
    places = [(tags[i : i + 1] == row).astype(BF16)[:, : n_lat * TILE] for i in range(3)]
    got = jnp.concatenate([part[...] for part in parts], axis=0)
    extra = got[:, width : width + half]
    total = tok_ref[...].reshape(n_tok, width).astype(F32) + matmul(places[0], got[:, :width])
    total = total + jnp.concatenate([matmul(place, extra) for place in places[1:]], axis=1)
    own_ref[...] = total.astype(BF16)
    grid = total.reshape(levels, rows, cols, width)
    for out_ref, part in (
        (north0_ref, grid[:, : rows - 1, :WIN]),
        (north1_ref, grid[:, : rows - 1, WIN:]),
        (east_ref, grid[:, :, :WIN]),
    ):
        out_ref[...] = part.reshape(out_ref.shape).astype(BF16)


def region_body(pick_ref, gain_ref, *refs):
    sources, (region_ref, normed_ref) = refs[:-2], refs[-2:]
    region = matmul(pick_ref[...], jnp.concatenate([ref[...] for ref in sources], axis=0))
    region_ref[...] = region.astype(BF16)
    centred = region - jnp.mean(region, axis=-1, keepdims=True)
    variance = jnp.mean(centred * centred, axis=-1, keepdims=True)
    normed_ref[...] = (centred * lax.rsqrt(variance + 1e-05) * gain_ref[...]).astype(BF16)


def block_start(part, k, n_lat, n_dp, d_blk):
    lat = lax.axis_index("lat") + k
    lat = jnp.where(lat >= n_lat, lat - n_lat, lat)
    dp = lax.axis_index("dp")
    dp = 1 - dp if part else dp
    return pl.multiple_of((lat * n_dp + dp) * d_blk, d_blk)


def attend_body(part, turns, n_lat, n_dp, normed_ref, wqkv_ref, shift_ref, out_ref):
    n_rows, width = normed_ref.shape
    n_tok = n_rows // 2
    d_blk = width // (n_lat * n_dp)
    starts = [block_start(part, k, n_lat, n_dp, d_blk) for k in turns]
    normed = normed_ref[...]
    thirds = []
    for third in range(3):
        weights = jnp.concatenate(
            [wqkv_ref[:, pl.ds(third * width + at, d_blk)] for at in starts], axis=1
        )
        thirds.append(matmul(normed, weights))
    scale = (d_blk // 2) ** (-0.5)
    queries = thirds[0].astype(BF16).astype(F32) * scale
    keys, values = thirds[1].astype(BF16), thirds[2].astype(BF16)
    key = iota((1, n_tok), 1)
    valid = lax.axis_index("lat") * WIN + key // WIN % WIN + shift_ref[:, :1] < WIN * n_lat
    first = iota((n_tok, d_blk), 1) < d_blk // 2
    ones = jnp.ones((n_tok, d_blk), BF16)
    for which in range(2):
        rows = slice(which * n_tok, (which + 1) * n_tok)
        for k in range(len(turns)):
            cols = slice(k * d_blk, (k + 1) * d_blk)
            query = queries[rows, cols]
            both = jnp.concatenate(
                [jnp.where(first, query, 0.0), jnp.where(first, 0.0, query)], axis=0
            ).astype(BF16)
            scores = lax.dot_general(
                both, keys[rows, cols], (((1,), (1,)), ((), ())), preferred_element_type=F32
            )
            scores = jnp.where(valid, scores, -1e30)
            powers = jnp.exp(scores - jnp.max(scores, axis=-1, keepdims=True)).astype(BF16)
            mixed = matmul(powers, jnp.concatenate([values[rows, cols], ones], axis=1))
            mixed = mixed[:, :d_blk] / mixed[:, d_blk:]
            out_ref[rows, cols] = jnp.where(first, mixed[:n_tok], mixed[n_tok:]).astype(BF16)


def turn_body(n_lon, cot_ref, other_ref, out_ref, flat_ref):
    _, levels, rows, cols, width = cot_ref.shape
    e_blk = width // n_lon
    n_tok = levels * rows * WIN
    here = lax.axis_index("lon")
    at = 0
    for ref in (cot_ref, other_ref):
        grid = ref[...].astype(F32).reshape(levels * rows, cols, width)
        for which in range(cols // WIN):
            flat_ref[...] = grid[:, which * WIN : (which + 1) * WIN].reshape(n_tok, width)
            for place, block in enumerate(reversed_order(n_lon)):
                lon = here ^ block
                piece = flat_ref[:, pl.ds(pl.multiple_of(lon * e_blk, e_blk), e_blk)]
                out_ref[place, :, at : at + n_tok] = piece.T.astype(BF16)
            at += n_tok


def reversed_order(count):
    bits = count.bit_length() - 1
    return [int(format(i, f"0{bits}b")[::-1], 2) if bits else 0 for i in range(count)]


def project_body(groups, n_lat, n_dp, reg_ref, wout_ref, *refs):
    ctx_refs, out_ref = refs[:-1], refs[-1]
    _, levels, rows, cols, width = out_ref.shape
    d_blk = width // (n_lat * n_dp)
    mixed = reg_ref[...].astype(F32)
    for (part, turns), ctx_ref in zip(groups, ctx_refs):
        starts = [block_start(part, k, n_lat, n_dp, d_blk) for k in turns]
        weights = jnp.concatenate([wout_ref[pl.ds(at, d_blk), :] for at in starts], axis=0)
        mixed = mixed + matmul(ctx_ref[...], weights)
    n_tok = levels * rows * WIN
    halves = [
        mixed[i * n_tok : (i + 1) * n_tok].reshape(levels * rows, WIN, width)
        for i in range(cols // WIN)
    ]
    out_ref[...] = jnp.concatenate(halves, axis=1).astype(BF16).reshape(out_ref.shape)


def gradient_body(cot_ref, mine_ref, other_ref, keep_ref, send_ref):
    context = jnp.concatenate([mine_ref[...], other_ref[...]], axis=0)
    count = cot_ref.shape[0] // 2
    for place in range(count):
        send_ref[place] = matmul(cot_ref[count + place], context).astype(BF16)
    for place in range(count):
        keep_ref[place] = matmul(cot_ref[place], context)


def in_hbm(array):
    return pltpu.with_memory_space_constraint(array, pltpu.HBM)


def fast_program(
    tokens, norm_gain, w_qkv, w_out, obs_vectors, obs_lat, obs_cell, obs_count, shift_offsets, cotangent
):
    _, levels, lat_dev, lon_dev, d_model = tokens.shape
    n_lat, n_lon, n_dp = (lax.axis_size(axis) for axis in ("lat", "lon", "dp"))
    shape = jax.ShapeDtypeStruct
    n_tok = levels * lat_dev * WIN
    n_rows = levels * lat_dev * lon_dev
    n_margin = levels * (lat_dev - 1) * WIN
    e_blk = d_model // n_lon
    d_blk = d_model // (n_lat * n_dp)
    dma = pltpu.SemaphoreType.DMA

    fetched = (obs_cell.reshape(1, -1), obs_lat.reshape(1, -1), obs_vectors)
    payload = call(
        functools.partial(route_body, n_lat),
        [shape((TILE, d_model + d_model // 2 + LANES), BF16)] * n_lat,
        (obs_count, *(in_hbm(array) for array in fetched)),
        [SMEM_SPEC] + [ANY_SPEC] * 3,
        "route",
        [*(pltpu.VMEM(array.shape, array.dtype) for array in fetched), dma((3,))],
    )
    arrived = [payload[0]] + [shifted(payload[k], "lat", k) for k in range(1, n_lat)]

    sizes = (n_rows, n_margin, n_margin, n_tok, n_margin)
    shift_offsets, tokens = lax.optimization_barrier((payload[0], shift_offsets, tokens))[1:]
    tokens, picks = call(
        functools.partial(stage_body, sizes),
        [shape(tokens.shape, BF16), shape((n_rows, sum(sizes)), BF16)],
        (shift_offsets, in_hbm(tokens)),
        [VMEM_SPEC, ANY_SPEC],
        "stage",
        [dma],
    )
    own, north0, north1, east = call(
        functools.partial(enrich_body, n_lat),
        [shape((n, d_model), BF16) for n in (n_rows, n_margin, n_margin, n_tok)],
        (tokens, *arrived),
        [VMEM_SPEC] * (1 + n_lat),
        "enrich",
    )
    loaded = (w_qkv, norm_gain.reshape(1, -1))
    loaded = lax.optimization_barrier((own, *loaded))[1:]
    w_qkv, gain = load(loaded, "weights")
    north0 = from_behind(north0, "lat", -1)
    north1 = from_behind(lax.optimization_barrier((north1, gain))[0], "lat", -1)
    east = shifted(east, "lon", -1)
    cot_other = swapped(cotangent, "dp", 1)
    corner = shifted(north0, "lon", -1)
    region, normed = call(
        region_body,
        [shape((n_rows, d_model), BF16)] * 2,
        (picks, gain, own, north0, north1, east, corner),
        [VMEM_SPEC] * 7,
        "region",
    )
    first, second = [k for k in range(n_lat) if k % 3], [k for k in range(n_lat) if k % 3 == 0]

    def attend(normed, part, turns):
        return call(
            functools.partial(attend_body, part, turns, n_lat, n_dp),
            shape((n_rows, len(turns) * d_blk), BF16),
            (normed, w_qkv, shift_offsets),
            [VMEM_SPEC] * 3,
            f"attend{part}{turns[0]}",
        )

    def local_gradient(turns, mine, other, cost):
        width = len(turns) * d_blk
        return call(
            gradient_body,
            [shape((n_lon // 2, e_blk, width), F32), shape((n_lon // 2, e_blk, width), BF16)],
            (cot_turned, mine, other),
            [VMEM_SPEC] * 3,
            f"gradient{turns[0]}",
            flops=cost,
        )

    def fold(kept, sent, bit):
        total = kept + swapped(sent, "lon", bit).astype(F32)
        middle = total.shape[0] // 2
        return (total[:middle], total[middle:].astype(BF16)) if middle else (total, None)

    def over_lon(kept, sent, bit):
        while bit < n_lon:
            kept, sent = fold(kept, sent, bit)
            bit *= 2
        return kept[0]

    def over_lat(total, turns):
        blocks = []
        for i, k in enumerate(turns):
            block = total[:, i * d_blk : (i + 1) * d_blk]
            blocks.append(shifted(block.astype(BF16), "lat", k).astype(F32) if k else block)
        return blocks

    def after(array, *others):
        return lax.optimization_barrier((array, *others))[0]

    cot_turned = call(
        functools.partial(turn_body, n_lon),
        shape((n_lon, e_blk, n_dp * n_rows), BF16),
        (cotangent, cot_other),
        [VMEM_SPEC] * 2,
        "turn",
        [pltpu.VMEM((n_tok, d_model), F32)],
    )
    theirs0 = attend(normed, 1, first)
    got0 = swapped(theirs0, "dp", 1)
    theirs1 = attend(after(normed, theirs0), 1, second)
    got1 = swapped(theirs1, "dp", 1)
    mine0 = attend(after(normed, theirs1), 0, first)
    mine1 = attend(after(normed, mine0), 0, second)
    kept0, sent0 = local_gradient(first, mine0, after(got0, mine1), 1)
    kept1, sent1 = local_gradient(second, mine1, after(got1, sent0), SLOW)
    total0 = over_lon(kept0, sent0, 1)
    total1 = over_lon(kept1, sent1, 1)
    blocks = over_lat(total0, first) + over_lat(total1, second)
    gradient = functools.reduce(jnp.add, blocks)
    groups = [(1, first), (0, first), (1, second), (0, second)]
    block_out = call(
        functools.partial(project_body, groups, n_lat, n_dp),
        shape((1, levels, lat_dev, lon_dev, d_model), BF16),
        (region, w_out, theirs0, mine0, theirs1, mine1),
        [VMEM_SPEC] * 6,
        "project",
    )
    return (block_out, gradient)


def on_device(tokens, norm_gain, w_qkv, w_out, obs_vectors, *rest):
    _, _, lat_dev, lon_dev, d_model = tokens.shape
    n_lat, n_lon, n_dp = (lax.axis_size(axis) for axis in ("lat", "lon", "dp"))
    cap = obs_vectors.shape[0] * 3 // (2 * n_lat)
    fits = (
        n_dp == 2
        and n_lon > 2
        and n_lon & (n_lon - 1) == 0
        and n_lat * TILE <= LANES
        and cap * 2 == TILE * 3
        and lat_dev == WIN
        and lon_dev == 2 * WIN
        and d_model // n_lon % LANES == 0
        and d_model // (n_lat * n_dp) == LANES
        and d_model // HEADS * 2 == LANES
    )
    program = fast_program if fits else general_program
    return program(tokens, norm_gain, w_qkv, w_out, obs_vectors, *rest)


def solution(mesh):
    placed = (
        P("dp", None, "lat", "lon", None),
        P(),
        P(),
        P(),
        P(("lon", "lat", "dp"), None),
        P(("lon", "lat", "dp"), None),
        P(("lon", "lat", "dp")),
        P(("lon", "lat", "dp")),
        P("dp", None),
        P("dp", None, "lat", "lon", None),
    )
    return jax.shard_map(
        on_device,
        mesh=mesh,
        in_specs=placed,
        out_specs=(P("dp", None, "lat", "lon", None), P("lon", ("lat", "dp"))),
        check_vma=False,
    )
```

```python
import functools

import jax
import jax.numpy as jnp
from jax import lax
from jax.experimental import pallas as pl
from jax.experimental.pallas import tpu as pltpu
from jax.sharding import PartitionSpec as P

HEADS = 16
WIN = 8
BF16 = jnp.bfloat16
F32 = jnp.float32
LANES = 128
TILE = 16
VMEM_LIMIT = 24 * 1024 * 1024
SLOW = 10**10


def from_behind(array, axis, by):
    devices = lax.axis_size(axis)
    pairs = [(i, i + by) for i in range(devices) if 0 <= i + by < devices]
    return lax.ppermute(array, axis, pairs)


def shifted(array, axis, by):
    devices = lax.axis_size(axis)
    return lax.ppermute(array, axis, [(i, (i + by) % devices) for i in range(devices)])


def swapped(array, axis, bit):
    devices = lax.axis_size(axis)
    return lax.ppermute(array, axis, [(i, i ^ bit) for i in range(devices)])


def to_windows(field_in):
    levels_n, rows_n, cols_n, feat_width = field_in.shape
    blocks = field_in.reshape(levels_n, rows_n // WIN, WIN, cols_n // WIN, WIN, feat_width)
    return blocks.transpose(1, 3, 0, 2, 4, 5).reshape(-1, levels_n * WIN * WIN, feat_width)


def from_windows(windows, levels_n, rows_n, cols_n):
    feat_width = windows.shape[-1]
    blocks = windows.reshape(rows_n // WIN, cols_n // WIN, levels_n, WIN, WIN, feat_width)
    return blocks.transpose(2, 0, 3, 1, 4, 5).reshape(levels_n, rows_n, cols_n, feat_width)


def window_block(win_tokens, win_valid, norm_gain, w_qkv, w_out):
    n_win, n_tok, d_model = win_tokens.shape
    head_dim = d_model // HEADS
    as_float = win_tokens.astype(F32)
    average = jnp.mean(as_float, axis=-1, keepdims=True)
    centred = as_float - average
    variance = jnp.mean(centred * centred, axis=-1, keepdims=True)
    normed = (centred * lax.rsqrt(variance + 1e-05) * norm_gain).astype(BF16)
    projected = jnp.dot(
        normed.reshape(-1, d_model), w_qkv, preferred_element_type=F32
    ).astype(BF16)
    projected = projected.reshape(n_win, n_tok, 3, HEADS, head_dim)
    queries = projected[:, :, 0]
    key_rows = projected[:, :, 1]
    values = projected[:, :, 2]
    scores = jnp.einsum(
        "wqhd,wkhd->whqk", queries, key_rows, preferred_element_type=F32
    ) * head_dim ** (-0.5)
    scores = jnp.where(win_valid[:, None, None, :], scores, -1e30)
    highest = jnp.max(scores, axis=-1, keepdims=True)
    powers = jnp.exp(scores - highest)
    weights = (powers / jnp.sum(powers, axis=-1, keepdims=True)).astype(BF16)
    context = jnp.einsum(
        "whqk,wkhd->wqhd", weights, values, preferred_element_type=F32
    ).astype(BF16)
    context = context.reshape(n_win, n_tok, d_model)
    result = jnp.dot(context.reshape(-1, d_model), w_out, preferred_element_type=F32)
    return ((as_float + result.reshape(n_win, n_tok, d_model)).astype(BF16), context)


def general_program(
    tokens, norm_gain, w_qkv, w_out, obs_vectors, obs_lat, obs_cell, obs_count, shift_offsets, cotangent
):
    n_batch, levels, lat_dev, lon_dev, d_model = tokens.shape
    n_lat = lax.axis_size("lat")
    obs_rows = obs_vectors.shape[0]
    capacity = obs_rows * 3 // (2 * n_lat)
    n_slots = n_lat * capacity
    destination = obs_lat[:, 0]
    one_hot = (destination[:, None] == jnp.arange(n_lat, dtype=jnp.int32)[None, :]).astype(jnp.int32)
    earlier = jnp.cumsum(one_hot, axis=0) - one_hot
    rank_in = jnp.sum(earlier * one_hot, axis=1)
    slot_of = destination * capacity + rank_in
    is_live = jnp.arange(obs_rows, dtype=jnp.int32) < obs_count[0]
    cell_tag = jnp.where(is_live, obs_cell, -1)
    chooser = slot_of[None, :] == jnp.arange(n_slots, dtype=jnp.int32)[:, None]
    sent_rows = (
        jnp.dot(chooser.astype(BF16), obs_vectors, preferred_element_type=F32)
        .astype(BF16)
        .reshape(n_lat, capacity, d_model)
    )
    sent_tags = (jnp.sum(chooser.astype(jnp.int32) * (cell_tag[None, :] + 1), axis=1) - 1).reshape(
        n_lat, capacity
    )
    got_rows, got_tags = (
        lax.all_to_all(sent_rows, "lat", split_axis=0, concat_axis=0, tiled=True),
        lax.all_to_all(sent_tags, "lat", split_axis=0, concat_axis=0, tiled=True),
    )
    flat_tokens = tokens.reshape(-1, d_model)
    placer = (
        got_tags.reshape(-1)[None, :] == jnp.arange(flat_tokens.shape[0], dtype=jnp.int32)[:, None]
    ).astype(BF16)
    added = jnp.dot(placer, got_rows.reshape(-1, d_model), preferred_element_type=F32)
    enriched = (flat_tokens.astype(F32) + added).astype(BF16).reshape(tokens.shape)
    margin = WIN - 1
    north_part = from_behind(enriched[:, :, :margin], "lat", -1)
    heightened = jnp.concatenate([enriched, north_part], axis=2)
    east_cols = shifted(heightened[:, :, :, :margin], "lon", -1)
    extended = jnp.concatenate([heightened, east_cols], axis=3)
    lat_shift = shift_offsets[0, 0]
    lon_shift = shift_offsets[0, 1]
    anchor = jnp.zeros((), jnp.int32)
    region = lax.dynamic_slice(
        extended, (anchor, anchor, lat_shift, lon_shift, anchor), tokens.shape
    )[0]
    source_rows = lax.axis_index("lat") * lat_dev + lat_shift + jnp.arange(lat_dev, dtype=jnp.int32)
    is_valid = jnp.broadcast_to(
        (source_rows < lat_dev * n_lat)[None, :, None, None], (levels, lat_dev, lon_dev, 1)
    )
    mixed, context = window_block(
        to_windows(region), to_windows(is_valid)[..., 0], norm_gain, w_qkv, w_out
    )
    block_out = from_windows(mixed, levels, lat_dev, lon_dev)[None]
    cot_rows = to_windows(cotangent[0]).reshape(-1, d_model)
    context_rows = context.reshape(-1, d_model)
    contract = (((0,), (0,)), ((), ()))
    partial_rows = lax.psum_scatter(
        lax.dot_general(cot_rows, context_rows, contract, preferred_element_type=F32),
        "lon",
        scatter_dimension=0,
        tiled=True,
    )
    gradient = lax.psum_scatter(partial_rows, ("lat", "dp"), scatter_dimension=1, tiled=True)
    return (block_out, gradient)


def call(body, out_shape, args, specs, name, scratch=(), flops=1, moved=1):
    return pl.pallas_call(
        body,
        out_shape=out_shape,
        in_specs=specs,
        out_specs=jax.tree.map(lambda _: pl.BlockSpec(memory_space=pltpu.VMEM), out_shape),
        scratch_shapes=list(scratch),
        compiler_params=pltpu.CompilerParams(vmem_limit_bytes=VMEM_LIMIT),
        cost_estimate=pl.CostEstimate(flops=flops, bytes_accessed=moved, transcendentals=0),
        name=name,
    )(*args)


VMEM_SPEC = pl.BlockSpec(memory_space=pltpu.VMEM)
SMEM_SPEC = pl.BlockSpec(memory_space=pltpu.SMEM)
ANY_SPEC = pl.BlockSpec(memory_space=pl.ANY)


def iota(shape, dim):
    return lax.broadcasted_iota(jnp.int32, shape, dim)


def over_rows(lhs, rhs):
    return lax.dot_general(lhs, rhs, (((0,), (0,)), ((), ())), preferred_element_type=F32)


def matmul(lhs, rhs):
    return jnp.dot(lhs, rhs, preferred_element_type=F32)


def copy_all(pairs, sems):
    copies = [pltpu.make_async_copy(src, dst, sems.at[i]) for i, (src, dst) in enumerate(pairs)]
    for copy in copies:
        copy.start()
    return copies


def route_body(n_lat, count_ref, cell_hbm, lat_hbm, vec_hbm, *refs):
    out_refs, (cell_ref, lat_ref, vec_ref, sems) = refs[:n_lat], refs[n_lat:]
    copies = copy_all([(cell_hbm, cell_ref), (lat_hbm, lat_ref), (vec_hbm, vec_ref)], sems)
    rows = vec_ref.shape[0]
    here = lax.axis_index("lat")
    lane = iota((rows, LANES), 1)
    below = (iota((rows, rows), 0) > iota((rows, rows), 1)).astype(BF16)
    same = iota((rows, rows), 0) == iota((rows, rows), 1)
    copies[0].wait()
    copies[1].wait()
    tag = jnp.where(iota((1, rows), 1) < count_ref[0], cell_ref[...] + 1, 0)
    tag, lat = (
        jnp.sum(jnp.where(same, field.astype(F32), 0.0), axis=1, keepdims=True)
        for field in (tag, lat_ref[...])
    )
    lat = lat.astype(jnp.int32)
    named = (lat == lane).astype(BF16)
    rank = jnp.sum(matmul(below, named) * named.astype(F32), axis=1, keepdims=True)
    rank = rank.astype(jnp.int32)
    base = jnp.where(lat < here, lat - here + n_lat, lat - here) * TILE
    late = rank >= TILE
    choosers = [
        (jnp.where(chosen, base + rank - back, -1) == lane).astype(BF16)
        for chosen, back in ((rank < TILE, 0), (late, TILE), (late, TILE // 2))
    ]
    tags = sum(
        over_rows(jnp.where(lane == base + i, tag, 0.0).astype(BF16), chooser)
        for i, chooser in enumerate(choosers)
    )
    copies[2].wait()
    width = vec_ref.shape[1]
    picked = over_rows(choosers[0], vec_ref[...])
    extra = over_rows(choosers[1], vec_ref[:, : width // 2])
    extra = extra + over_rows(choosers[2], vec_ref[:, width // 2 :])
    for k, out_ref in enumerate(out_refs):
        piece = slice(k * TILE, (k + 1) * TILE)
        out_ref[:, :width] = picked[piece].astype(BF16)
        out_ref[:, width : width + width // 2] = extra[piece].astype(BF16)
        out_ref[:, width + width // 2 :] = tags[piece].astype(BF16)


def load_body(*refs):
    count = len(refs) // 2
    for copy in copy_all(list(zip(refs[:count], refs[count:-1])), refs[-1]):
        copy.wait()


def load(arrays, name):
    return call(
        load_body,
        [jax.ShapeDtypeStruct(array.shape, array.dtype) for array in arrays],
        tuple(in_hbm(array) for array in arrays),
        [ANY_SPEC] * len(arrays),
        name,
        [pltpu.SemaphoreType.DMA((len(arrays),))],
    )


def stage_body(sizes, shift_ref, tok_hbm, tok_ref, pick_ref, sem):
    copy = pltpu.make_async_copy(tok_hbm, tok_ref, sem)
    copy.start()
    lat_shift, lon_shift = shift_ref[:, :1], shift_ref[:, 1:]
    n_rows, n_cols = pick_ref.shape
    n_tok = n_rows // 2
    row = iota((n_rows, 1), 0)
    level = row // (WIN * WIN) % (n_tok // (WIN * WIN))
    at_lat = row // WIN % WIN + lat_shift
    at_lon = row % WIN + row // n_tok * WIN + lon_shift
    cols, margin = 2 * WIN, WIN - 1
    starts = [sum(sizes[:i]) for i in range(len(sizes))]
    inside = (level * WIN + at_lat) * cols + at_lon
    north = (level * margin + at_lat - WIN) * WIN + at_lon % WIN
    east = (level * WIN + at_lat) * WIN + at_lon - cols
    index = jnp.where(
        at_lat < WIN,
        jnp.where(at_lon < cols, inside, east + starts[3]),
        north + jnp.where(at_lon < WIN, starts[1], jnp.where(at_lon < cols, starts[2], starts[4])),
    )
    pick_ref[...] = (index == iota((n_rows, n_cols), 1)).astype(BF16)
    copy.wait()


def enrich_body(n_lat, tok_ref, *refs):
    parts, (own_ref, north0_ref, north1_ref, east_ref) = refs[:n_lat], refs[n_lat:]
    _, levels, rows, cols, width = tok_ref.shape
    n_tok = levels * rows * cols
    half = width // 2
    tags = sum(part[:, width + half :].astype(F32) for part in parts).astype(jnp.int32)
    row = iota((n_tok, LANES), 0) + 1
    places = [(tags[i : i + 1] == row).astype(BF16)[:, : n_lat * TILE] for i in range(3)]
    got = jnp.concatenate([part[...] for part in parts], axis=0)
    extra = got[:, width : width + half]
    total = tok_ref[...].reshape(n_tok, width).astype(F32) + matmul(places[0], got[:, :width])
    total = total + jnp.concatenate([matmul(place, extra) for place in places[1:]], axis=1)
    own_ref[...] = total.astype(BF16)
    grid = total.reshape(levels, rows, cols, width)
    for out_ref, part in (
        (north0_ref, grid[:, : rows - 1, :WIN]),
        (north1_ref, grid[:, : rows - 1, WIN:]),
        (east_ref, grid[:, :, :WIN]),
    ):
        out_ref[...] = part.reshape(out_ref.shape).astype(BF16)


def region_body(pick_ref, gain_ref, *refs):
    sources, (region_ref, normed_ref) = refs[:-2], refs[-2:]
    region = matmul(pick_ref[...], jnp.concatenate([ref[...] for ref in sources], axis=0))
    region_ref[...] = region.astype(BF16)
    centred = region - jnp.mean(region, axis=-1, keepdims=True)
    variance = jnp.mean(centred * centred, axis=-1, keepdims=True)
    normed_ref[...] = (centred * lax.rsqrt(variance + 1e-05) * gain_ref[...]).astype(BF16)


def block_start(part, k, n_lat, n_dp, d_blk):
    lat = lax.axis_index("lat") + k
    lat = jnp.where(lat >= n_lat, lat - n_lat, lat)
    dp = lax.axis_index("dp")
    dp = 1 - dp if part else dp
    return pl.multiple_of((lat * n_dp + dp) * d_blk, d_blk)


def attend_body(part, turns, n_lat, n_dp, normed_ref, wqkv_ref, shift_ref, out_ref):
    n_rows, width = normed_ref.shape
    n_tok = n_rows // 2
    d_blk = width // (n_lat * n_dp)
    starts = [block_start(part, k, n_lat, n_dp, d_blk) for k in turns]
    normed = normed_ref[...]
    thirds = []
    for third in range(3):
        weights = jnp.concatenate(
            [wqkv_ref[:, pl.ds(third * width + at, d_blk)] for at in starts], axis=1
        )
        thirds.append(matmul(normed, weights))
    scale = (d_blk // 2) ** (-0.5)
    queries = thirds[0].astype(BF16).astype(F32) * scale
    keys, values = thirds[1].astype(BF16), thirds[2].astype(BF16)
    key = iota((1, n_tok), 1)
    valid = lax.axis_index("lat") * WIN + key // WIN % WIN + shift_ref[:, :1] < WIN * n_lat
    first = iota((n_tok, d_blk), 1) < d_blk // 2
    ones = jnp.ones((n_tok, d_blk), BF16)
    for which in range(2):
        rows = slice(which * n_tok, (which + 1) * n_tok)
        for k in range(len(turns)):
            cols = slice(k * d_blk, (k + 1) * d_blk)
            query = queries[rows, cols]
            both = jnp.concatenate(
                [jnp.where(first, query, 0.0), jnp.where(first, 0.0, query)], axis=0
            ).astype(BF16)
            scores = lax.dot_general(
                both, keys[rows, cols], (((1,), (1,)), ((), ())), preferred_element_type=F32
            )
            scores = jnp.where(valid, scores, -1e30)
            powers = jnp.exp(scores - jnp.max(scores, axis=-1, keepdims=True)).astype(BF16)
            mixed = matmul(powers, jnp.concatenate([values[rows, cols], ones], axis=1))
            mixed = mixed[:, :d_blk] / mixed[:, d_blk:]
            out_ref[rows, cols] = jnp.where(first, mixed[:n_tok], mixed[n_tok:]).astype(BF16)


def turn_body(n_lon, cot_ref, other_ref, out_ref, flat_ref):
    _, levels, rows, cols, width = cot_ref.shape
    e_blk = width // n_lon
    n_tok = levels * rows * WIN
    here = lax.axis_index("lon")
    at = 0
    for ref in (cot_ref, other_ref):
        grid = ref[...].astype(F32).reshape(levels * rows, cols, width)
        for which in range(cols // WIN):
            flat_ref[...] = grid[:, which * WIN : (which + 1) * WIN].reshape(n_tok, width)
            for place, block in enumerate(reversed_order(n_lon)):
                lon = here ^ block
                piece = flat_ref[:, pl.ds(pl.multiple_of(lon * e_blk, e_blk), e_blk)]
                out_ref[place, :, at : at + n_tok] = piece.T.astype(BF16)
            at += n_tok


def reversed_order(count):
    bits = count.bit_length() - 1
    return [int(format(i, f"0{bits}b")[::-1], 2) if bits else 0 for i in range(count)]


def project_body(groups, n_lat, n_dp, reg_ref, wout_ref, *refs):
    ctx_refs, out_ref = refs[:-1], refs[-1]
    _, levels, rows, cols, width = out_ref.shape
    d_blk = width // (n_lat * n_dp)
    mixed = reg_ref[...].astype(F32)
    for (part, turns), ctx_ref in zip(groups, ctx_refs):
        starts = [block_start(part, k, n_lat, n_dp, d_blk) for k in turns]
        weights = jnp.concatenate([wout_ref[pl.ds(at, d_blk), :] for at in starts], axis=0)
        mixed = mixed + matmul(ctx_ref[...], weights)
    n_tok = levels * rows * WIN
    halves = [
        mixed[i * n_tok : (i + 1) * n_tok].reshape(levels * rows, WIN, width)
        for i in range(cols // WIN)
    ]
    out_ref[...] = jnp.concatenate(halves, axis=1).astype(BF16).reshape(out_ref.shape)


def gradient_body(cot_ref, mine_ref, other_ref, keep_ref, send_ref):
    context = jnp.concatenate([mine_ref[...], other_ref[...]], axis=0)
    count = cot_ref.shape[0] // 2
    for place in range(count):
        send_ref[place] = matmul(cot_ref[count + place], context).astype(BF16)
    for place in range(count):
        keep_ref[place] = matmul(cot_ref[place], context)


def in_hbm(array):
    return pltpu.with_memory_space_constraint(array, pltpu.HBM)


def fast_program(
    tokens, norm_gain, w_qkv, w_out, obs_vectors, obs_lat, obs_cell, obs_count, shift_offsets, cotangent
):
    _, levels, lat_dev, lon_dev, d_model = tokens.shape
    n_lat, n_lon, n_dp = (lax.axis_size(axis) for axis in ("lat", "lon", "dp"))
    shape = jax.ShapeDtypeStruct
    n_tok = levels * lat_dev * WIN
    n_rows = levels * lat_dev * lon_dev
    n_margin = levels * (lat_dev - 1) * WIN
    e_blk = d_model // n_lon
    d_blk = d_model // (n_lat * n_dp)
    dma = pltpu.SemaphoreType.DMA

    fetched = (obs_cell.reshape(1, -1), obs_lat.reshape(1, -1), obs_vectors)
    payload = call(
        functools.partial(route_body, n_lat),
        [shape((TILE, d_model + d_model // 2 + LANES), BF16)] * n_lat,
        (obs_count, *(in_hbm(array) for array in fetched)),
        [SMEM_SPEC] + [ANY_SPEC] * 3,
        "route",
        [*(pltpu.VMEM(array.shape, array.dtype) for array in fetched), dma((3,))],
    )
    arrived = [payload[0]] + [shifted(payload[k], "lat", k) for k in range(1, n_lat)]

    sizes = (n_rows, n_margin, n_margin, n_tok, n_margin)
    shift_offsets, tokens = lax.optimization_barrier((payload[0], shift_offsets, tokens))[1:]
    tokens, picks = call(
        functools.partial(stage_body, sizes),
        [shape(tokens.shape, BF16), shape((n_rows, sum(sizes)), BF16)],
        (shift_offsets, in_hbm(tokens)),
        [VMEM_SPEC, ANY_SPEC],
        "stage",
        [dma],
    )
    own, north0, north1, east = call(
        functools.partial(enrich_body, n_lat),
        [shape((n, d_model), BF16) for n in (n_rows, n_margin, n_margin, n_tok)],
        (tokens, *arrived),
        [VMEM_SPEC] * (1 + n_lat),
        "enrich",
    )
    north0 = from_behind(north0, "lat", -1)
    north1 = from_behind(north1, "lat", -1)
    east = shifted(east, "lon", -1)
    cot_other = swapped(cotangent, "dp", 1)
    corner = shifted(north0, "lon", -1)
    loaded = (w_qkv, w_out, norm_gain.reshape(1, -1))
    loaded = lax.optimization_barrier((north0, *loaded))[1:]
    w_qkv, w_out, gain = load(loaded, "weights")
    region, normed = call(
        region_body,
        [shape((n_rows, d_model), BF16)] * 2,
        (picks, gain, own, north0, north1, east, corner),
        [VMEM_SPEC] * 7,
        "region",
    )
    first, second = [k for k in range(n_lat) if k % 3], [k for k in range(n_lat) if k % 3 == 0]

    def attend(normed, part, turns):
        return call(
            functools.partial(attend_body, part, turns, n_lat, n_dp),
            shape((n_rows, len(turns) * d_blk), BF16),
            (normed, w_qkv, shift_offsets),
            [VMEM_SPEC] * 3,
            f"attend{part}{turns[0]}",
            flops=SLOW if (part, turns) == (0, second) else 1,
        )

    def local_gradient(turns, mine, other, cost):
        width = len(turns) * d_blk
        return call(
            gradient_body,
            [shape((n_lon // 2, e_blk, width), F32), shape((n_lon // 2, e_blk, width), BF16)],
            (cot_turned, mine, other),
            [VMEM_SPEC] * 3,
            f"gradient{turns[0]}",
            flops=cost,
        )

    def halves(total):
        middle = total.shape[0] // 2
        return total[:middle], total[middle:].astype(BF16)

    def fold(kept, sent, bit):
        return kept + swapped(sent, "lon", bit).astype(F32)

    def over_lon(total, bit):
        while bit < n_lon:
            total = fold(*halves(total), bit)
            bit *= 2
        return total

    def over_lat(total, turns):
        blocks = []
        for i, k in enumerate(turns):
            block = total[..., i * d_blk : (i + 1) * d_blk]
            blocks.append(shifted(block.astype(BF16), "lat", k).astype(F32) if k else block)
        return functools.reduce(jnp.add, blocks)

    def after(array, *others):
        return lax.optimization_barrier((array, *others))[0]

    cot_turned = call(
        functools.partial(turn_body, n_lon),
        shape((n_lon, e_blk, n_dp * n_rows), BF16),
        (cotangent, cot_other),
        [VMEM_SPEC] * 2,
        "turn",
        [pltpu.VMEM((n_tok, d_model), F32)],
    )
    theirs0 = attend(normed, 1, first)
    got0 = swapped(theirs0, "dp", 1)
    theirs1 = attend(after(normed, theirs0), 1, second)
    got1 = swapped(theirs1, "dp", 1)
    mine0 = attend(after(normed, theirs1), 0, first)
    kept0, sent0 = local_gradient(first, mine0, got0, 1)
    mine1 = attend(after(normed, sent0), 0, second)
    kept0, sent0 = halves(fold(after(kept0, mine1), sent0, 1))
    kept1, sent1 = local_gradient(second, mine1, after(got1, sent0), SLOW)
    kept1, sent1 = halves(fold(kept1, sent1, 1))
    groups = [(1, first), (0, first), (1, second), (0, second)]
    block_out = call(
        functools.partial(project_body, groups, n_lat, n_dp),
        shape((1, levels, lat_dev, lon_dev, d_model), BF16),
        (after(region, sent0), w_out, theirs0, mine0, theirs1, mine1),
        [VMEM_SPEC] * 6,
        "project",
        flops=SLOW,
    )
    total0 = fold(after(kept0, block_out, sent1), sent0, 2)
    total1 = fold(kept1, sent1, 2)
    gradient = over_lat(over_lon(total0, 4), first)
    gradient, total1 = lax.optimization_barrier((gradient, over_lat(over_lon(total1, 4), second)))
    gradient = (gradient + total1)[0]
    return (block_out, gradient)


def on_device(tokens, norm_gain, w_qkv, w_out, obs_vectors, *rest):
    _, _, lat_dev, lon_dev, d_model = tokens.shape
    n_lat, n_lon, n_dp = (lax.axis_size(axis) for axis in ("lat", "lon", "dp"))
    cap = obs_vectors.shape[0] * 3 // (2 * n_lat)
    fits = (
        n_dp == 2
        and n_lon > 2
        and n_lon & (n_lon - 1) == 0
        and n_lat * TILE <= LANES
        and cap * 2 == TILE * 3
        and lat_dev == WIN
        and lon_dev == 2 * WIN
        and d_model // n_lon % LANES == 0
        and d_model // (n_lat * n_dp) == LANES
        and d_model // HEADS * 2 == LANES
    )
    program = fast_program if fits else general_program
    return program(tokens, norm_gain, w_qkv, w_out, obs_vectors, *rest)


def solution(mesh):
    placed = (
        P("dp", None, "lat", "lon", None),
        P(),
        P(),
        P(),
        P(("lon", "lat", "dp"), None),
        P(("lon", "lat", "dp"), None),
        P(("lon", "lat", "dp")),
        P(("lon", "lat", "dp")),
        P("dp", None),
        P("dp", None, "lat", "lon", None),
    )
    return jax.shard_map(
        on_device,
        mesh=mesh,
        in_specs=placed,
        out_specs=(P("dp", None, "lat", "lon", None), P("lon", ("lat", "dp"))),
        check_vma=False,
    )
```

```python
import functools

import jax
import jax.numpy as jnp
from jax import lax
from jax.experimental import pallas as pl
from jax.experimental.pallas import tpu as pltpu
from jax.sharding import PartitionSpec as P

HEADS = 16
WIN = 8
BF16 = jnp.bfloat16
F32 = jnp.float32
LANES = 128
TILE = 16
VMEM_LIMIT = 24 * 1024 * 1024
SLOW = 10**10


def from_behind(array, axis, by):
    devices = lax.axis_size(axis)
    pairs = [(i, i + by) for i in range(devices) if 0 <= i + by < devices]
    return lax.ppermute(array, axis, pairs)


def shifted(array, axis, by):
    devices = lax.axis_size(axis)
    return lax.ppermute(array, axis, [(i, (i + by) % devices) for i in range(devices)])


def swapped(array, axis, bit):
    devices = lax.axis_size(axis)
    return lax.ppermute(array, axis, [(i, i ^ bit) for i in range(devices)])


def to_windows(field_in):
    levels_n, rows_n, cols_n, feat_width = field_in.shape
    blocks = field_in.reshape(levels_n, rows_n // WIN, WIN, cols_n // WIN, WIN, feat_width)
    return blocks.transpose(1, 3, 0, 2, 4, 5).reshape(-1, levels_n * WIN * WIN, feat_width)


def from_windows(windows, levels_n, rows_n, cols_n):
    feat_width = windows.shape[-1]
    blocks = windows.reshape(rows_n // WIN, cols_n // WIN, levels_n, WIN, WIN, feat_width)
    return blocks.transpose(2, 0, 3, 1, 4, 5).reshape(levels_n, rows_n, cols_n, feat_width)


def window_block(win_tokens, win_valid, norm_gain, w_qkv, w_out):
    n_win, n_tok, d_model = win_tokens.shape
    head_dim = d_model // HEADS
    as_float = win_tokens.astype(F32)
    average = jnp.mean(as_float, axis=-1, keepdims=True)
    centred = as_float - average
    variance = jnp.mean(centred * centred, axis=-1, keepdims=True)
    normed = (centred * lax.rsqrt(variance + 1e-05) * norm_gain).astype(BF16)
    projected = jnp.dot(
        normed.reshape(-1, d_model), w_qkv, preferred_element_type=F32
    ).astype(BF16)
    projected = projected.reshape(n_win, n_tok, 3, HEADS, head_dim)
    queries = projected[:, :, 0]
    key_rows = projected[:, :, 1]
    values = projected[:, :, 2]
    scores = jnp.einsum(
        "wqhd,wkhd->whqk", queries, key_rows, preferred_element_type=F32
    ) * head_dim ** (-0.5)
    scores = jnp.where(win_valid[:, None, None, :], scores, -1e30)
    highest = jnp.max(scores, axis=-1, keepdims=True)
    powers = jnp.exp(scores - highest)
    weights = (powers / jnp.sum(powers, axis=-1, keepdims=True)).astype(BF16)
    context = jnp.einsum(
        "whqk,wkhd->wqhd", weights, values, preferred_element_type=F32
    ).astype(BF16)
    context = context.reshape(n_win, n_tok, d_model)
    result = jnp.dot(context.reshape(-1, d_model), w_out, preferred_element_type=F32)
    return ((as_float + result.reshape(n_win, n_tok, d_model)).astype(BF16), context)


def general_program(
    tokens, norm_gain, w_qkv, w_out, obs_vectors, obs_lat, obs_cell, obs_count, shift_offsets, cotangent
):
    n_batch, levels, lat_dev, lon_dev, d_model = tokens.shape
    n_lat = lax.axis_size("lat")
    obs_rows = obs_vectors.shape[0]
    capacity = obs_rows * 3 // (2 * n_lat)
    n_slots = n_lat * capacity
    destination = obs_lat[:, 0]
    one_hot = (destination[:, None] == jnp.arange(n_lat, dtype=jnp.int32)[None, :]).astype(jnp.int32)
    earlier = jnp.cumsum(one_hot, axis=0) - one_hot
    rank_in = jnp.sum(earlier * one_hot, axis=1)
    slot_of = destination * capacity + rank_in
    is_live = jnp.arange(obs_rows, dtype=jnp.int32) < obs_count[0]
    cell_tag = jnp.where(is_live, obs_cell, -1)
    chooser = slot_of[None, :] == jnp.arange(n_slots, dtype=jnp.int32)[:, None]
    sent_rows = (
        jnp.dot(chooser.astype(BF16), obs_vectors, preferred_element_type=F32)
        .astype(BF16)
        .reshape(n_lat, capacity, d_model)
    )
    sent_tags = (jnp.sum(chooser.astype(jnp.int32) * (cell_tag[None, :] + 1), axis=1) - 1).reshape(
        n_lat, capacity
    )
    got_rows, got_tags = (
        lax.all_to_all(sent_rows, "lat", split_axis=0, concat_axis=0, tiled=True),
        lax.all_to_all(sent_tags, "lat", split_axis=0, concat_axis=0, tiled=True),
    )
    flat_tokens = tokens.reshape(-1, d_model)
    placer = (
        got_tags.reshape(-1)[None, :] == jnp.arange(flat_tokens.shape[0], dtype=jnp.int32)[:, None]
    ).astype(BF16)
    added = jnp.dot(placer, got_rows.reshape(-1, d_model), preferred_element_type=F32)
    enriched = (flat_tokens.astype(F32) + added).astype(BF16).reshape(tokens.shape)
    margin = WIN - 1
    north_part = from_behind(enriched[:, :, :margin], "lat", -1)
    heightened = jnp.concatenate([enriched, north_part], axis=2)
    east_cols = shifted(heightened[:, :, :, :margin], "lon", -1)
    extended = jnp.concatenate([heightened, east_cols], axis=3)
    lat_shift = shift_offsets[0, 0]
    lon_shift = shift_offsets[0, 1]
    anchor = jnp.zeros((), jnp.int32)
    region = lax.dynamic_slice(
        extended, (anchor, anchor, lat_shift, lon_shift, anchor), tokens.shape
    )[0]
    source_rows = lax.axis_index("lat") * lat_dev + lat_shift + jnp.arange(lat_dev, dtype=jnp.int32)
    is_valid = jnp.broadcast_to(
        (source_rows < lat_dev * n_lat)[None, :, None, None], (levels, lat_dev, lon_dev, 1)
    )
    mixed, context = window_block(
        to_windows(region), to_windows(is_valid)[..., 0], norm_gain, w_qkv, w_out
    )
    block_out = from_windows(mixed, levels, lat_dev, lon_dev)[None]
    cot_rows = to_windows(cotangent[0]).reshape(-1, d_model)
    context_rows = context.reshape(-1, d_model)
    contract = (((0,), (0,)), ((), ()))
    partial_rows = lax.psum_scatter(
        lax.dot_general(cot_rows, context_rows, contract, preferred_element_type=F32),
        "lon",
        scatter_dimension=0,
        tiled=True,
    )
    gradient = lax.psum_scatter(partial_rows, ("lat", "dp"), scatter_dimension=1, tiled=True)
    return (block_out, gradient)


def call(body, out_shape, args, specs, name, scratch=(), flops=1, moved=1):
    return pl.pallas_call(
        body,
        out_shape=out_shape,
        in_specs=specs,
        out_specs=jax.tree.map(lambda _: pl.BlockSpec(memory_space=pltpu.VMEM), out_shape),
        scratch_shapes=list(scratch),
        compiler_params=pltpu.CompilerParams(vmem_limit_bytes=VMEM_LIMIT),
        cost_estimate=pl.CostEstimate(flops=flops, bytes_accessed=moved, transcendentals=0),
        name=name,
    )(*args)


VMEM_SPEC = pl.BlockSpec(memory_space=pltpu.VMEM)
SMEM_SPEC = pl.BlockSpec(memory_space=pltpu.SMEM)
ANY_SPEC = pl.BlockSpec(memory_space=pl.ANY)


def iota(shape, dim):
    return lax.broadcasted_iota(jnp.int32, shape, dim)


def matmul(lhs, rhs):
    return jnp.dot(lhs, rhs, preferred_element_type=F32)


def copy_all(pairs, sems):
    copies = [pltpu.make_async_copy(src, dst, sems.at[i]) for i, (src, dst) in enumerate(pairs)]
    for copy in copies:
        copy.start()
    return copies


def route_body(n_lat, count_ref, cell_hbm, lat_hbm, vec_hbm, *refs):
    out_refs, (cell_ref, lat_ref, vec_ref, sems) = refs[:n_lat], refs[n_lat:]
    copies = copy_all([(cell_hbm, cell_ref), (lat_hbm, lat_ref), (vec_hbm, vec_ref)], sems)
    rows = vec_ref.shape[0]
    here = lax.axis_index("lat")
    above = (iota((rows, rows), 0) < iota((rows, rows), 1)).astype(BF16)
    slot = iota((LANES, rows), 0)
    copies[0].wait()
    copies[1].wait()
    tag = jnp.where(iota((1, rows), 1) < count_ref[0], cell_ref[...] + 1, 0).astype(F32)
    lat = lat_ref[...]
    named = (iota((TILE, rows), 0) == lat).astype(BF16)
    rank = jnp.sum(matmul(named, above) * named.astype(F32), axis=0, keepdims=True)
    rank = rank.astype(jnp.int32)
    base = jnp.where(lat < here, lat - here + n_lat, lat - here) * TILE
    late = rank >= TILE
    choosers = [
        (slot == jnp.where(chosen, base + rank - back, -1)).astype(BF16)
        for chosen, back in ((rank < TILE, 0), (late, TILE), (late, TILE // 2))
    ]
    tags = sum(
        lax.dot_general(
            jnp.where(slot == base + i, tag, 0.0).astype(BF16),
            chooser,
            (((1,), (1,)), ((), ())),
            preferred_element_type=F32,
        )
        for i, chooser in enumerate(choosers)
    )
    copies[2].wait()
    width = vec_ref.shape[1]
    picked = matmul(choosers[0], vec_ref[...])
    extra = matmul(choosers[1], vec_ref[:, : width // 2])
    extra = extra + matmul(choosers[2], vec_ref[:, width // 2 :])
    for k, out_ref in enumerate(out_refs):
        piece = slice(k * TILE, (k + 1) * TILE)
        out_ref[:, :width] = picked[piece].astype(BF16)
        out_ref[:, width : width + width // 2] = extra[piece].astype(BF16)
        out_ref[:, width + width // 2 :] = tags[piece].astype(BF16)


def load_body(*refs):
    count = len(refs) // 2
    for copy in copy_all(list(zip(refs[:count], refs[count:-1])), refs[-1]):
        copy.wait()


def load(arrays, name):
    return call(
        load_body,
        [jax.ShapeDtypeStruct(array.shape, array.dtype) for array in arrays],
        tuple(in_hbm(array) for array in arrays),
        [ANY_SPEC] * len(arrays),
        name,
        [pltpu.SemaphoreType.DMA((len(arrays),))],
    )


def stage_body(sizes, shift_ref, tok_hbm, tok_ref, pick_ref, sem):
    copy = pltpu.make_async_copy(tok_hbm, tok_ref, sem)
    copy.start()
    lat_shift, lon_shift = shift_ref[:, :1], shift_ref[:, 1:]
    n_rows, n_cols = pick_ref.shape
    n_tok = n_rows // 2
    row = iota((n_rows, 1), 0)
    level = row // (WIN * WIN) % (n_tok // (WIN * WIN))
    at_lat = row // WIN % WIN + lat_shift
    at_lon = row % WIN + row // n_tok * WIN + lon_shift
    cols, margin = 2 * WIN, WIN - 1
    starts = [sum(sizes[:i]) for i in range(len(sizes))]
    inside = (level * WIN + at_lat) * cols + at_lon
    north = (level * margin + at_lat - WIN) * WIN + at_lon % WIN
    east = (level * WIN + at_lat) * WIN + at_lon - cols
    index = jnp.where(
        at_lat < WIN,
        jnp.where(at_lon < cols, inside, east + starts[3]),
        north + jnp.where(at_lon < WIN, starts[1], jnp.where(at_lon < cols, starts[2], starts[4])),
    )
    pick_ref[...] = (index == iota((n_rows, n_cols), 1)).astype(BF16)
    copy.wait()


def enrich_body(n_lat, tok_ref, *refs):
    parts, (own_ref, north0_ref, north1_ref, east_ref) = refs[:n_lat], refs[n_lat:]
    _, levels, rows, cols, width = tok_ref.shape
    n_tok = levels * rows * cols
    half = width // 2
    tags = sum(part[:, width + half :].astype(F32) for part in parts).astype(jnp.int32)
    row = iota((n_tok, LANES), 0) + 1
    places = [(tags[i : i + 1] == row).astype(BF16)[:, : n_lat * TILE] for i in range(3)]
    got = jnp.concatenate([part[...] for part in parts], axis=0)
    extra = got[:, width : width + half]
    total = tok_ref[...].reshape(n_tok, width).astype(F32) + matmul(places[0], got[:, :width])
    total = total + jnp.concatenate([matmul(place, extra) for place in places[1:]], axis=1)
    own_ref[...] = total.astype(BF16)
    grid = total.reshape(levels, rows, cols, width)
    for out_ref, part in (
        (north0_ref, grid[:, : rows - 1, :WIN]),
        (north1_ref, grid[:, : rows - 1, WIN:]),
        (east_ref, grid[:, :, :WIN]),
    ):
        out_ref[...] = part.reshape(out_ref.shape).astype(BF16)


def region_body(pick_ref, gain_ref, *refs):
    sources, (region_ref, normed_ref) = refs[:-2], refs[-2:]
    region = matmul(pick_ref[...], jnp.concatenate([ref[...] for ref in sources], axis=0))
    region_ref[...] = region.astype(BF16)
    centred = region - jnp.mean(region, axis=-1, keepdims=True)
    variance = jnp.mean(centred * centred, axis=-1, keepdims=True)
    normed_ref[...] = (centred * lax.rsqrt(variance + 1e-05) * gain_ref[...]).astype(BF16)


def block_start(part, k, n_lat, n_dp, d_blk):
    lat = lax.axis_index("lat") + k
    lat = jnp.where(lat >= n_lat, lat - n_lat, lat)
    dp = lax.axis_index("dp")
    dp = 1 - dp if part else dp
    return pl.multiple_of((lat * n_dp + dp) * d_blk, d_blk)


def attend_body(part, turns, n_lat, n_dp, normed_ref, wqkv_ref, shift_ref, out_ref):
    n_rows, width = normed_ref.shape
    n_tok = n_rows // 2
    d_blk = width // (n_lat * n_dp)
    starts = [block_start(part, k, n_lat, n_dp, d_blk) for k in turns]
    normed = normed_ref[...]
    thirds = []
    for third in range(3):
        weights = jnp.concatenate(
            [wqkv_ref[:, pl.ds(third * width + at, d_blk)] for at in starts], axis=1
        )
        thirds.append(matmul(normed, weights))
    scale = (d_blk // 2) ** (-0.5)
    queries = (thirds[0].astype(BF16).astype(F32) * scale).astype(BF16)
    keys, values = thirds[1].astype(BF16), thirds[2].astype(BF16)
    key = iota((1, n_tok), 1)
    valid = lax.axis_index("lat") * WIN + key // WIN % WIN + shift_ref[:, :1] < WIN * n_lat
    first = iota((n_tok, d_blk), 1) < d_blk // 2
    ones, none = jnp.ones((n_tok, d_blk), BF16), jnp.zeros((n_tok, d_blk), BF16)
    units = [
        (slice(which * n_tok, (which + 1) * n_tok), slice(k * d_blk, (k + 1) * d_blk))
        for which in range(2)
        for k in range(len(turns))
    ]
    scores = []
    for unit in units:
        query = queries[unit]
        both = jnp.concatenate(
            [jnp.where(first, query, none), jnp.where(first, none, query)], axis=0
        )
        scores.append(
            lax.dot_general(both, keys[unit], (((1,), (1,)), ((), ())), preferred_element_type=F32)
        )
    scores = [jnp.where(valid, score, -1e30) for score in scores]
    highest = [jnp.max(score, axis=-1, keepdims=True) for score in scores]
    powers = [jnp.exp(score - top).astype(BF16) for score, top in zip(scores, highest)]
    mixed = [
        matmul(power, jnp.concatenate([values[unit], ones], axis=1))
        for power, unit in zip(powers, units)
    ]
    for context, unit in zip(mixed, units):
        context = context[:, :d_blk] / context[:, d_blk:]
        out_ref[unit] = jnp.where(first, context[:n_tok], context[n_tok:]).astype(BF16)


def turn_body(n_lon, cot_ref, other_ref, out_ref, flat_ref):
    _, levels, rows, cols, width = cot_ref.shape
    e_blk = width // n_lon
    n_tok = levels * rows * WIN
    here = lax.axis_index("lon")
    at = 0
    for ref in (cot_ref, other_ref):
        grid = ref[...].astype(F32).reshape(levels * rows, cols, width)
        for which in range(cols // WIN):
            flat_ref[...] = grid[:, which * WIN : (which + 1) * WIN].reshape(n_tok, width)
            for place, block in enumerate(reversed_order(n_lon)):
                lon = here ^ block
                piece = flat_ref[:, pl.ds(pl.multiple_of(lon * e_blk, e_blk), e_blk)]
                out_ref[place, :, at : at + n_tok] = piece.T.astype(BF16)
            at += n_tok


def reversed_order(count):
    bits = count.bit_length() - 1
    return [int(format(i, f"0{bits}b")[::-1], 2) if bits else 0 for i in range(count)]


def project_body(groups, n_lat, n_dp, reg_ref, wout_ref, *refs):
    ctx_refs, out_ref = refs[:-1], refs[-1]
    _, levels, rows, cols, width = out_ref.shape
    d_blk = width // (n_lat * n_dp)
    mixed = reg_ref[...].astype(F32)
    for (part, turns), ctx_ref in zip(groups, ctx_refs):
        starts = [block_start(part, k, n_lat, n_dp, d_blk) for k in turns]
        weights = jnp.concatenate([wout_ref[pl.ds(at, d_blk), :] for at in starts], axis=0)
        mixed = mixed + matmul(ctx_ref[...], weights)
    n_tok = levels * rows * WIN
    halves = [
        mixed[i * n_tok : (i + 1) * n_tok].reshape(levels * rows, WIN, width)
        for i in range(cols // WIN)
    ]
    out_ref[...] = jnp.concatenate(halves, axis=1).astype(BF16).reshape(out_ref.shape)


def gradient_body(cot_ref, mine_ref, other_ref, keep_ref, send_ref):
    context = jnp.concatenate([mine_ref[...], other_ref[...]], axis=0)
    count = cot_ref.shape[0] // 2
    for place in range(count):
        send_ref[place] = matmul(cot_ref[count + place], context).astype(BF16)
    for place in range(count):
        keep_ref[place] = matmul(cot_ref[place], context)


def in_hbm(array):
    return pltpu.with_memory_space_constraint(array, pltpu.HBM)


def fast_program(
    tokens, norm_gain, w_qkv, w_out, obs_vectors, obs_lat, obs_cell, obs_count, shift_offsets, cotangent
):
    _, levels, lat_dev, lon_dev, d_model = tokens.shape
    n_lat, n_lon, n_dp = (lax.axis_size(axis) for axis in ("lat", "lon", "dp"))
    shape = jax.ShapeDtypeStruct
    n_tok = levels * lat_dev * WIN
    n_rows = levels * lat_dev * lon_dev
    n_margin = levels * (lat_dev - 1) * WIN
    e_blk = d_model // n_lon
    d_blk = d_model // (n_lat * n_dp)
    dma = pltpu.SemaphoreType.DMA

    fetched = (obs_cell.reshape(1, -1), obs_lat.reshape(1, -1), obs_vectors)
    payload = call(
        functools.partial(route_body, n_lat),
        [shape((TILE, d_model + d_model // 2 + LANES), BF16)] * n_lat,
        (obs_count, *(in_hbm(array) for array in fetched)),
        [SMEM_SPEC] + [ANY_SPEC] * 3,
        "route",
        [*(pltpu.VMEM(array.shape, array.dtype) for array in fetched), dma((3,))],
    )
    arrived = [payload[0]] + [shifted(payload[k], "lat", k) for k in range(1, n_lat)]

    sizes = (n_rows, n_margin, n_margin, n_tok, n_margin)
    shift_offsets, tokens = lax.optimization_barrier((payload[0], shift_offsets, tokens))[1:]
    tokens, picks = call(
        functools.partial(stage_body, sizes),
        [shape(tokens.shape, BF16), shape((n_rows, sum(sizes)), BF16)],
        (shift_offsets, in_hbm(tokens)),
        [VMEM_SPEC, ANY_SPEC],
        "stage",
        [dma],
    )
    own, north0, north1, east = call(
        functools.partial(enrich_body, n_lat),
        [shape((n, d_model), BF16) for n in (n_rows, n_margin, n_margin, n_tok)],
        (tokens, *arrived),
        [VMEM_SPEC] * (1 + n_lat),
        "enrich",
    )
    north0 = from_behind(north0, "lat", -1)
    north1 = from_behind(north1, "lat", -1)
    east = shifted(east, "lon", -1)
    cot_other = swapped(cotangent, "dp", 1)
    corner = shifted(north0, "lon", -1)
    loaded = (w_qkv, w_out, norm_gain.reshape(1, -1))
    loaded = lax.optimization_barrier((north0, *loaded))[1:]
    w_qkv, w_out, gain = load(loaded, "weights")
    region, normed = call(
        region_body,
        [shape((n_rows, d_model), BF16)] * 2,
        (picks, gain, own, north0, north1, east, corner),
        [VMEM_SPEC] * 7,
        "region",
    )
    first, second = [k for k in range(n_lat) if k % 3], [k for k in range(n_lat) if k % 3 == 0]

    def attend(normed, part, turns):
        return call(
            functools.partial(attend_body, part, turns, n_lat, n_dp),
            shape((n_rows, len(turns) * d_blk), BF16),
            (normed, w_qkv, shift_offsets),
            [VMEM_SPEC] * 3,
            f"attend{part}{turns[0]}",
            flops=SLOW if (part, turns) == (0, second) else 1,
        )

    def local_gradient(turns, mine, other, cost):
        width = len(turns) * d_blk
        return call(
            gradient_body,
            [shape((n_lon // 2, e_blk, width), F32), shape((n_lon // 2, e_blk, width), BF16)],
            (cot_turned, mine, other),
            [VMEM_SPEC] * 3,
            f"gradient{turns[0]}",
            flops=cost,
        )

    def halves(total):
        middle = total.shape[0] // 2
        return total[:middle], total[middle:].astype(BF16)

    def fold(kept, sent, bit):
        return kept + swapped(sent, "lon", bit).astype(F32)

    def over_lon(total, bit):
        while bit < n_lon:
            total = fold(*halves(total), bit)
            bit *= 2
        return total

    def over_lat(total, turns):
        blocks = []
        for i, k in enumerate(turns):
            block = total[..., i * d_blk : (i + 1) * d_blk]
            blocks.append(shifted(block.astype(BF16), "lat", k).astype(F32) if k else block)
        return functools.reduce(jnp.add, blocks)

    def after(array, *others):
        return lax.optimization_barrier((array, *others))[0]

    cot_turned = call(
        functools.partial(turn_body, n_lon),
        shape((n_lon, e_blk, n_dp * n_rows), BF16),
        (cotangent, cot_other),
        [VMEM_SPEC] * 2,
        "turn",
        [pltpu.VMEM((n_tok, d_model), F32)],
    )
    theirs0 = attend(normed, 1, first)
    got0 = swapped(theirs0, "dp", 1)
    mine0 = attend(after(normed, theirs0), 0, first)
    theirs1 = attend(after(normed, mine0), 1, second)
    got1 = swapped(theirs1, "dp", 1)
    kept0, sent0 = local_gradient(first, mine0, after(got0, theirs1), 1)
    mine1 = attend(after(normed, sent0), 0, second)
    kept0, sent0 = halves(fold(after(kept0, mine1), sent0, 1))
    kept1, sent1 = local_gradient(second, mine1, after(got1, sent0), SLOW)
    kept1, sent1 = halves(fold(kept1, sent1, 1))
    groups = [(1, first), (0, first), (1, second), (0, second)]
    block_out = call(
        functools.partial(project_body, groups, n_lat, n_dp),
        shape((1, levels, lat_dev, lon_dev, d_model), BF16),
        (after(region, sent0), w_out, theirs0, mine0, theirs1, mine1),
        [VMEM_SPEC] * 6,
        "project",
        flops=SLOW,
    )
    total0 = fold(after(kept0, block_out, sent1), sent0, 2)
    total1 = fold(kept1, sent1, 2)
    gradient = over_lat(over_lon(total0, 4), first)
    gradient, total1 = lax.optimization_barrier((gradient, over_lat(over_lon(total1, 4), second)))
    gradient = (gradient + total1)[0]
    return (block_out, gradient)


def on_device(tokens, norm_gain, w_qkv, w_out, obs_vectors, *rest):
    _, _, lat_dev, lon_dev, d_model = tokens.shape
    n_lat, n_lon, n_dp = (lax.axis_size(axis) for axis in ("lat", "lon", "dp"))
    cap = obs_vectors.shape[0] * 3 // (2 * n_lat)
    fits = (
        n_dp == 2
        and n_lon > 2
        and n_lon & (n_lon - 1) == 0
        and n_lat * TILE <= LANES
        and n_lat <= TILE
        and cap * 2 == TILE * 3
        and lat_dev == WIN
        and lon_dev == 2 * WIN
        and d_model // n_lon % LANES == 0
        and d_model // (n_lat * n_dp) == LANES
        and d_model // HEADS * 2 == LANES
    )
    program = fast_program if fits else general_program
    return program(tokens, norm_gain, w_qkv, w_out, obs_vectors, *rest)


def solution(mesh):
    placed = (
        P("dp", None, "lat", "lon", None),
        P(),
        P(),
        P(),
        P(("lon", "lat", "dp"), None),
        P(("lon", "lat", "dp"), None),
        P(("lon", "lat", "dp")),
        P(("lon", "lat", "dp")),
        P("dp", None),
        P("dp", None, "lat", "lon", None),
    )
    return jax.shard_map(
        on_device,
        mesh=mesh,
        in_specs=placed,
        out_specs=(P("dp", None, "lat", "lon", None), P("lon", ("lat", "dp"))),
        check_vma=False,
    )
```

```python
import functools

import jax
import jax.numpy as jnp
from jax import lax
from jax.experimental import pallas as pl
from jax.experimental.pallas import tpu as pltpu
from jax.sharding import PartitionSpec as P

HEADS = 16
WIN = 8
BF16 = jnp.bfloat16
F32 = jnp.float32
LANES = 128
TILE = 16
VMEM_LIMIT = 24 * 1024 * 1024
SLOW = 10**10


def from_behind(array, axis, by):
    devices = lax.axis_size(axis)
    pairs = [(i, i + by) for i in range(devices) if 0 <= i + by < devices]
    return lax.ppermute(array, axis, pairs)


def shifted(array, axis, by):
    devices = lax.axis_size(axis)
    return lax.ppermute(array, axis, [(i, (i + by) % devices) for i in range(devices)])


def swapped(array, axis, bit):
    devices = lax.axis_size(axis)
    return lax.ppermute(array, axis, [(i, i ^ bit) for i in range(devices)])


def to_windows(field_in):
    levels_n, rows_n, cols_n, feat_width = field_in.shape
    blocks = field_in.reshape(levels_n, rows_n // WIN, WIN, cols_n // WIN, WIN, feat_width)
    return blocks.transpose(1, 3, 0, 2, 4, 5).reshape(-1, levels_n * WIN * WIN, feat_width)


def from_windows(windows, levels_n, rows_n, cols_n):
    feat_width = windows.shape[-1]
    blocks = windows.reshape(rows_n // WIN, cols_n // WIN, levels_n, WIN, WIN, feat_width)
    return blocks.transpose(2, 0, 3, 1, 4, 5).reshape(levels_n, rows_n, cols_n, feat_width)


def window_block(win_tokens, win_valid, norm_gain, w_qkv, w_out):
    n_win, n_tok, d_model = win_tokens.shape
    head_dim = d_model // HEADS
    as_float = win_tokens.astype(F32)
    average = jnp.mean(as_float, axis=-1, keepdims=True)
    centred = as_float - average
    variance = jnp.mean(centred * centred, axis=-1, keepdims=True)
    normed = (centred * lax.rsqrt(variance + 1e-05) * norm_gain).astype(BF16)
    projected = jnp.dot(
        normed.reshape(-1, d_model), w_qkv, preferred_element_type=F32
    ).astype(BF16)
    projected = projected.reshape(n_win, n_tok, 3, HEADS, head_dim)
    queries = projected[:, :, 0]
    key_rows = projected[:, :, 1]
    values = projected[:, :, 2]
    scores = jnp.einsum(
        "wqhd,wkhd->whqk", queries, key_rows, preferred_element_type=F32
    ) * head_dim ** (-0.5)
    scores = jnp.where(win_valid[:, None, None, :], scores, -1e30)
    highest = jnp.max(scores, axis=-1, keepdims=True)
    powers = jnp.exp(scores - highest)
    weights = (powers / jnp.sum(powers, axis=-1, keepdims=True)).astype(BF16)
    context = jnp.einsum(
        "whqk,wkhd->wqhd", weights, values, preferred_element_type=F32
    ).astype(BF16)
    context = context.reshape(n_win, n_tok, d_model)
    result = jnp.dot(context.reshape(-1, d_model), w_out, preferred_element_type=F32)
    return ((as_float + result.reshape(n_win, n_tok, d_model)).astype(BF16), context)


def general_program(
    tokens, norm_gain, w_qkv, w_out, obs_vectors, obs_lat, obs_cell, obs_count, shift_offsets, cotangent
):
    n_batch, levels, lat_dev, lon_dev, d_model = tokens.shape
    n_lat = lax.axis_size("lat")
    obs_rows = obs_vectors.shape[0]
    capacity = obs_rows * 3 // (2 * n_lat)
    n_slots = n_lat * capacity
    destination = obs_lat[:, 0]
    one_hot = (destination[:, None] == jnp.arange(n_lat, dtype=jnp.int32)[None, :]).astype(jnp.int32)
    earlier = jnp.cumsum(one_hot, axis=0) - one_hot
    rank_in = jnp.sum(earlier * one_hot, axis=1)
    slot_of = destination * capacity + rank_in
    is_live = jnp.arange(obs_rows, dtype=jnp.int32) < obs_count[0]
    cell_tag = jnp.where(is_live, obs_cell, -1)
    chooser = slot_of[None, :] == jnp.arange(n_slots, dtype=jnp.int32)[:, None]
    sent_rows = (
        jnp.dot(chooser.astype(BF16), obs_vectors, preferred_element_type=F32)
        .astype(BF16)
        .reshape(n_lat, capacity, d_model)
    )
    sent_tags = (jnp.sum(chooser.astype(jnp.int32) * (cell_tag[None, :] + 1), axis=1) - 1).reshape(
        n_lat, capacity
    )
    got_rows, got_tags = (
        lax.all_to_all(sent_rows, "lat", split_axis=0, concat_axis=0, tiled=True),
        lax.all_to_all(sent_tags, "lat", split_axis=0, concat_axis=0, tiled=True),
    )
    flat_tokens = tokens.reshape(-1, d_model)
    placer = (
        got_tags.reshape(-1)[None, :] == jnp.arange(flat_tokens.shape[0], dtype=jnp.int32)[:, None]
    ).astype(BF16)
    added = jnp.dot(placer, got_rows.reshape(-1, d_model), preferred_element_type=F32)
    enriched = (flat_tokens.astype(F32) + added).astype(BF16).reshape(tokens.shape)
    margin = WIN - 1
    north_part = from_behind(enriched[:, :, :margin], "lat", -1)
    heightened = jnp.concatenate([enriched, north_part], axis=2)
    east_cols = shifted(heightened[:, :, :, :margin], "lon", -1)
    extended = jnp.concatenate([heightened, east_cols], axis=3)
    lat_shift = shift_offsets[0, 0]
    lon_shift = shift_offsets[0, 1]
    anchor = jnp.zeros((), jnp.int32)
    region = lax.dynamic_slice(
        extended, (anchor, anchor, lat_shift, lon_shift, anchor), tokens.shape
    )[0]
    source_rows = lax.axis_index("lat") * lat_dev + lat_shift + jnp.arange(lat_dev, dtype=jnp.int32)
    is_valid = jnp.broadcast_to(
        (source_rows < lat_dev * n_lat)[None, :, None, None], (levels, lat_dev, lon_dev, 1)
    )
    mixed, context = window_block(
        to_windows(region), to_windows(is_valid)[..., 0], norm_gain, w_qkv, w_out
    )
    block_out = from_windows(mixed, levels, lat_dev, lon_dev)[None]
    cot_rows = to_windows(cotangent[0]).reshape(-1, d_model)
    context_rows = context.reshape(-1, d_model)
    contract = (((0,), (0,)), ((), ()))
    partial_rows = lax.psum_scatter(
        lax.dot_general(cot_rows, context_rows, contract, preferred_element_type=F32),
        "lon",
        scatter_dimension=0,
        tiled=True,
    )
    gradient = lax.psum_scatter(partial_rows, ("lat", "dp"), scatter_dimension=1, tiled=True)
    return (block_out, gradient)


def call(body, out_shape, args, specs, name, scratch=(), flops=1, moved=1):
    return pl.pallas_call(
        body,
        out_shape=out_shape,
        in_specs=specs,
        out_specs=jax.tree.map(lambda _: pl.BlockSpec(memory_space=pltpu.VMEM), out_shape),
        scratch_shapes=list(scratch),
        compiler_params=pltpu.CompilerParams(vmem_limit_bytes=VMEM_LIMIT),
        cost_estimate=pl.CostEstimate(flops=flops, bytes_accessed=moved, transcendentals=0),
        name=name,
    )(*args)


VMEM_SPEC = pl.BlockSpec(memory_space=pltpu.VMEM)
SMEM_SPEC = pl.BlockSpec(memory_space=pltpu.SMEM)
ANY_SPEC = pl.BlockSpec(memory_space=pl.ANY)


def iota(shape, dim):
    return lax.broadcasted_iota(jnp.int32, shape, dim)


def matmul(lhs, rhs):
    return jnp.dot(lhs, rhs, preferred_element_type=F32)


def copy_all(pairs, sems):
    copies = [pltpu.make_async_copy(src, dst, sems.at[i]) for i, (src, dst) in enumerate(pairs)]
    for copy in copies:
        copy.start()
    return copies


def above_body(above_ref):
    above_ref[...] = (iota(above_ref.shape, 0) < iota(above_ref.shape, 1)).astype(BF16)


def live_body(count_ref, live_ref):
    live_ref[...] = (iota(live_ref.shape, 1) < count_ref[0]).astype(jnp.int32)


def route_body(n_lat, above_ref, live_ref, cell_ref, lat_ref, vec_ref, *out_refs):
    rows = vec_ref.shape[0]
    here = lax.axis_index("lat")
    slot = iota((LANES, rows), 0)
    tag = (live_ref[...] * (cell_ref[...] + 1)).astype(F32)
    lat = lat_ref[...]
    named = (iota((TILE, rows), 0) == lat).astype(BF16)
    rank = jnp.sum(matmul(named, above_ref[...]) * named.astype(F32), axis=0, keepdims=True)
    rank = rank.astype(jnp.int32)
    base = jnp.where(lat < here, lat - here + n_lat, lat - here) * TILE
    late = rank >= TILE
    choosers = [
        (slot == jnp.where(chosen, base + rank - back, -1)).astype(BF16)
        for chosen, back in ((rank < TILE, 0), (late, TILE), (late, TILE // 2))
    ]
    tags = sum(
        lax.dot_general(
            jnp.where(slot == base + i, tag, 0.0).astype(BF16),
            chooser,
            (((1,), (1,)), ((), ())),
            preferred_element_type=F32,
        )
        for i, chooser in enumerate(choosers)
    )
    width = vec_ref.shape[1]
    picked = matmul(choosers[0], vec_ref[...])
    extra = matmul(choosers[1], vec_ref[:, : width // 2])
    extra = extra + matmul(choosers[2], vec_ref[:, width // 2 :])
    for k, out_ref in enumerate(out_refs):
        piece = slice(k * TILE, (k + 1) * TILE)
        out_ref[:, :width] = picked[piece].astype(BF16)
        out_ref[:, width : width + width // 2] = extra[piece].astype(BF16)
        out_ref[:, width + width // 2 :] = tags[piece].astype(BF16)


def load_body(*refs):
    count = len(refs) // 2
    for copy in copy_all(list(zip(refs[:count], refs[count:-1])), refs[-1]):
        copy.wait()


def load(arrays, name):
    return call(
        load_body,
        [jax.ShapeDtypeStruct(array.shape, array.dtype) for array in arrays],
        tuple(in_hbm(array) for array in arrays),
        [ANY_SPEC] * len(arrays),
        name,
        [pltpu.SemaphoreType.DMA((len(arrays),))],
    )


def stage_body(sizes, shift_ref, tok_hbm, tok_ref, pick_ref, sem):
    copy = pltpu.make_async_copy(tok_hbm, tok_ref, sem)
    copy.start()
    lat_shift, lon_shift = shift_ref[:, :1], shift_ref[:, 1:]
    n_rows, n_cols = pick_ref.shape
    n_tok = n_rows // 2
    row = iota((n_rows, 1), 0)
    level = row // (WIN * WIN) % (n_tok // (WIN * WIN))
    at_lat = row // WIN % WIN + lat_shift
    at_lon = row % WIN + row // n_tok * WIN + lon_shift
    cols, margin = 2 * WIN, WIN - 1
    starts = [sum(sizes[:i]) for i in range(len(sizes))]
    inside = (level * WIN + at_lat) * cols + at_lon
    north = (level * margin + at_lat - WIN) * WIN + at_lon % WIN
    east = (level * WIN + at_lat) * WIN + at_lon - cols
    index = jnp.where(
        at_lat < WIN,
        jnp.where(at_lon < cols, inside, east + starts[3]),
        north + jnp.where(at_lon < WIN, starts[1], jnp.where(at_lon < cols, starts[2], starts[4])),
    )
    pick_ref[...] = (index == iota((n_rows, n_cols), 1)).astype(BF16)
    copy.wait()


def enrich_body(n_lat, tok_ref, *refs):
    parts, (own_ref, north0_ref, north1_ref, east_ref) = refs[:n_lat], refs[n_lat:]
    _, levels, rows, cols, width = tok_ref.shape
    n_tok = levels * rows * cols
    half = width // 2
    tags = sum(part[:, width + half :].astype(F32) for part in parts).astype(jnp.int32)
    row = iota((n_tok, LANES), 0) + 1
    places = [(tags[i : i + 1] == row).astype(BF16)[:, : n_lat * TILE] for i in range(3)]
    got = jnp.concatenate([part[...] for part in parts], axis=0)
    extra = got[:, width : width + half]
    total = tok_ref[...].reshape(n_tok, width).astype(F32) + matmul(places[0], got[:, :width])
    total = total + jnp.concatenate([matmul(place, extra) for place in places[1:]], axis=1)
    own_ref[...] = total.astype(BF16)
    grid = total.reshape(levels, rows, cols, width)
    for out_ref, part in (
        (north0_ref, grid[:, : rows - 1, :WIN]),
        (north1_ref, grid[:, : rows - 1, WIN:]),
        (east_ref, grid[:, :, :WIN]),
    ):
        out_ref[...] = part.reshape(out_ref.shape).astype(BF16)


def region_body(pick_ref, gain_ref, *refs):
    sources, (region_ref, normed_ref) = refs[:-2], refs[-2:]
    region = matmul(pick_ref[...], jnp.concatenate([ref[...] for ref in sources], axis=0))
    region_ref[...] = region.astype(BF16)
    centred = region - jnp.mean(region, axis=-1, keepdims=True)
    variance = jnp.mean(centred * centred, axis=-1, keepdims=True)
    normed_ref[...] = (centred * lax.rsqrt(variance + 1e-05) * gain_ref[...]).astype(BF16)


def block_start(part, k, n_lat, n_dp, d_blk):
    lat = lax.axis_index("lat") + k
    lat = jnp.where(lat >= n_lat, lat - n_lat, lat)
    dp = lax.axis_index("dp")
    dp = 1 - dp if part else dp
    return pl.multiple_of((lat * n_dp + dp) * d_blk, d_blk)


def attend_body(part, turns, n_lat, n_dp, normed_ref, wqkv_ref, shift_ref, out_ref):
    n_rows, width = normed_ref.shape
    n_tok = n_rows // 2
    d_blk = width // (n_lat * n_dp)
    starts = [block_start(part, k, n_lat, n_dp, d_blk) for k in turns]
    normed = normed_ref[...]
    thirds = []
    for third in range(3):
        weights = jnp.concatenate(
            [wqkv_ref[:, pl.ds(third * width + at, d_blk)] for at in starts], axis=1
        )
        thirds.append(matmul(normed, weights))
    scale = (d_blk // 2) ** (-0.5)
    queries = (thirds[0].astype(BF16).astype(F32) * scale).astype(BF16)
    keys, values = thirds[1].astype(BF16), thirds[2].astype(BF16)
    key = iota((1, n_tok), 1)
    valid = lax.axis_index("lat") * WIN + key // WIN % WIN + shift_ref[:, :1] < WIN * n_lat
    first = iota((n_tok, d_blk), 1) < d_blk // 2
    ones, none = jnp.ones((n_tok, d_blk), BF16), jnp.zeros((n_tok, d_blk), BF16)
    units = [
        (slice(which * n_tok, (which + 1) * n_tok), slice(k * d_blk, (k + 1) * d_blk))
        for which in range(2)
        for k in range(len(turns))
    ]
    scores = []
    for unit in units:
        query = queries[unit]
        both = jnp.concatenate(
            [jnp.where(first, query, none), jnp.where(first, none, query)], axis=0
        )
        scores.append(
            lax.dot_general(both, keys[unit], (((1,), (1,)), ((), ())), preferred_element_type=F32)
        )
    scores = [jnp.where(valid, score, -1e30) for score in scores]
    highest = [jnp.max(score, axis=-1, keepdims=True) for score in scores]
    powers = [jnp.exp(score - top).astype(BF16) for score, top in zip(scores, highest)]
    mixed = [
        matmul(power, jnp.concatenate([values[unit], ones], axis=1))
        for power, unit in zip(powers, units)
    ]
    for context, unit in zip(mixed, units):
        context = context[:, :d_blk] / context[:, d_blk:]
        out_ref[unit] = jnp.where(first, context[:n_tok], context[n_tok:]).astype(BF16)


def turn_body(n_lon, cot_ref, other_ref, out_ref, flat_ref):
    _, levels, rows, cols, width = cot_ref.shape
    e_blk = width // n_lon
    n_tok = levels * rows * WIN
    here = lax.axis_index("lon")
    at = 0
    for ref in (cot_ref, other_ref):
        grid = ref[...].astype(F32).reshape(levels * rows, cols, width)
        for which in range(cols // WIN):
            flat_ref[...] = grid[:, which * WIN : (which + 1) * WIN].reshape(n_tok, width)
            for place, block in enumerate(reversed_order(n_lon)):
                lon = here ^ block
                piece = flat_ref[:, pl.ds(pl.multiple_of(lon * e_blk, e_blk), e_blk)]
                out_ref[place, :, at : at + n_tok] = piece.T.astype(BF16)
            at += n_tok


def reversed_order(count):
    bits = count.bit_length() - 1
    return [int(format(i, f"0{bits}b")[::-1], 2) if bits else 0 for i in range(count)]


def project_body(groups, n_lat, n_dp, reg_ref, wout_ref, *refs):
    ctx_refs, out_ref = refs[:-1], refs[-1]
    _, levels, rows, cols, width = out_ref.shape
    d_blk = width // (n_lat * n_dp)
    mixed = reg_ref[...].astype(F32)
    for (part, turns), ctx_ref in zip(groups, ctx_refs):
        starts = [block_start(part, k, n_lat, n_dp, d_blk) for k in turns]
        weights = jnp.concatenate([wout_ref[pl.ds(at, d_blk), :] for at in starts], axis=0)
        mixed = mixed + matmul(ctx_ref[...], weights)
    n_tok = levels * rows * WIN
    halves = [
        mixed[i * n_tok : (i + 1) * n_tok].reshape(levels * rows, WIN, width)
        for i in range(cols // WIN)
    ]
    out_ref[...] = jnp.concatenate(halves, axis=1).astype(BF16).reshape(out_ref.shape)


def gradient_body(cot_ref, mine_ref, other_ref, keep_ref, send_ref):
    context = jnp.concatenate([mine_ref[...], other_ref[...]], axis=0)
    count = cot_ref.shape[0] // 2
    for place in range(count):
        send_ref[place] = matmul(cot_ref[count + place], context).astype(BF16)
    for place in range(count):
        keep_ref[place] = matmul(cot_ref[place], context)


def in_hbm(array):
    return pltpu.with_memory_space_constraint(array, pltpu.HBM)


def fast_program(
    tokens, norm_gain, w_qkv, w_out, obs_vectors, obs_lat, obs_cell, obs_count, shift_offsets, cotangent
):
    _, levels, lat_dev, lon_dev, d_model = tokens.shape
    n_lat, n_lon, n_dp = (lax.axis_size(axis) for axis in ("lat", "lon", "dp"))
    shape = jax.ShapeDtypeStruct
    n_tok = levels * lat_dev * WIN
    n_rows = levels * lat_dev * lon_dev
    n_margin = levels * (lat_dev - 1) * WIN
    e_blk = d_model // n_lon
    d_blk = d_model // (n_lat * n_dp)
    dma = pltpu.SemaphoreType.DMA

    fetched = (obs_cell.reshape(1, -1), obs_lat.reshape(1, -1), obs_vectors)
    obs_rows = obs_vectors.shape[0]
    above = call(above_body, shape((obs_rows, obs_rows), BF16), (), [], "above", flops=SLOW)
    above, obs_count = lax.optimization_barrier((above, obs_count))
    live = call(
        live_body,
        shape(fetched[0].shape, jnp.int32),
        (obs_count,),
        [SMEM_SPEC],
        "live",
    )
    payload = call(
        functools.partial(route_body, n_lat),
        [shape((TILE, d_model + d_model // 2 + LANES), BF16)] * n_lat,
        (above, live, *fetched),
        [VMEM_SPEC] * 5,
        "route",
    )
    arrived = [payload[0]] + [shifted(payload[k], "lat", k) for k in range(1, n_lat)]

    sizes = (n_rows, n_margin, n_margin, n_tok, n_margin)
    shift_offsets, tokens = lax.optimization_barrier((payload[0], shift_offsets, tokens))[1:]
    tokens, picks = call(
        functools.partial(stage_body, sizes),
        [shape(tokens.shape, BF16), shape((n_rows, sum(sizes)), BF16)],
        (shift_offsets, in_hbm(tokens)),
        [VMEM_SPEC, ANY_SPEC],
        "stage",
        [dma],
    )
    own, north0, north1, east = call(
        functools.partial(enrich_body, n_lat),
        [shape((n, d_model), BF16) for n in (n_rows, n_margin, n_margin, n_tok)],
        (tokens, *arrived),
        [VMEM_SPEC] * (1 + n_lat),
        "enrich",
    )
    north0 = from_behind(north0, "lat", -1)
    north1 = from_behind(north1, "lat", -1)
    east = shifted(east, "lon", -1)
    cot_other = swapped(cotangent, "dp", 1)
    corner = shifted(north0, "lon", -1)
    loaded = (w_qkv, w_out, norm_gain.reshape(1, -1))
    loaded = lax.optimization_barrier((north0, *loaded))[1:]
    w_qkv, w_out, gain = load(loaded, "weights")
    region, normed = call(
        region_body,
        [shape((n_rows, d_model), BF16)] * 2,
        (picks, gain, own, north0, north1, east, corner),
        [VMEM_SPEC] * 7,
        "region",
    )
    first, second = [k for k in range(n_lat) if k % 3], [k for k in range(n_lat) if k % 3 == 0]

    def attend(normed, part, turns):
        return call(
            functools.partial(attend_body, part, turns, n_lat, n_dp),
            shape((n_rows, len(turns) * d_blk), BF16),
            (normed, w_qkv, shift_offsets),
            [VMEM_SPEC] * 3,
            f"attend{part}{turns[0]}",
            flops=SLOW if (part, turns) == (0, second) else 1,
        )

    def local_gradient(turns, mine, other, cost):
        width = len(turns) * d_blk
        return call(
            gradient_body,
            [shape((n_lon // 2, e_blk, width), F32), shape((n_lon // 2, e_blk, width), BF16)],
            (cot_turned, mine, other),
            [VMEM_SPEC] * 3,
            f"gradient{turns[0]}",
            flops=cost,
        )

    def halves(total):
        middle = total.shape[0] // 2
        return total[:middle], total[middle:].astype(BF16)

    def fold(kept, sent, bit):
        return kept + swapped(sent, "lon", bit).astype(F32)

    def over_lon(total, bit):
        while bit < n_lon:
            total = fold(*halves(total), bit)
            bit *= 2
        return total

    def over_lat(total, turns):
        blocks = []
        for i, k in enumerate(turns):
            block = total[..., i * d_blk : (i + 1) * d_blk]
            blocks.append(shifted(block.astype(BF16), "lat", k).astype(F32) if k else block)
        return functools.reduce(jnp.add, blocks)

    def after(array, *others):
        return lax.optimization_barrier((array, *others))[0]

    cot_turned = call(
        functools.partial(turn_body, n_lon),
        shape((n_lon, e_blk, n_dp * n_rows), BF16),
        (cotangent, cot_other),
        [VMEM_SPEC] * 2,
        "turn",
        [pltpu.VMEM((n_tok, d_model), F32)],
    )
    theirs0 = attend(normed, 1, first)
    got0 = swapped(theirs0, "dp", 1)
    mine0 = attend(after(normed, theirs0), 0, first)
    theirs1 = attend(after(normed, mine0), 1, second)
    got1 = swapped(theirs1, "dp", 1)
    kept0, sent0 = local_gradient(first, mine0, after(got0, theirs1), 1)
    mine1 = attend(after(normed, sent0), 0, second)
    kept0, sent0 = halves(fold(after(kept0, mine1), sent0, 1))
    kept1, sent1 = local_gradient(second, mine1, after(got1, sent0), SLOW)
    kept1, sent1 = halves(fold(kept1, sent1, 1))
    groups = [(1, first), (0, first), (1, second), (0, second)]
    block_out = call(
        functools.partial(project_body, groups, n_lat, n_dp),
        shape((1, levels, lat_dev, lon_dev, d_model), BF16),
        (after(region, sent0), w_out, theirs0, mine0, theirs1, mine1),
        [VMEM_SPEC] * 6,
        "project",
        flops=SLOW,
    )
    total0 = fold(after(kept0, block_out, sent1), sent0, 2)
    total1 = fold(kept1, sent1, 2)
    gradient = over_lat(over_lon(total0, 4), first)
    gradient, total1 = lax.optimization_barrier((gradient, over_lat(over_lon(total1, 4), second)))
    gradient = (gradient + total1)[0]
    return (block_out, gradient)


def on_device(tokens, norm_gain, w_qkv, w_out, obs_vectors, *rest):
    _, _, lat_dev, lon_dev, d_model = tokens.shape
    n_lat, n_lon, n_dp = (lax.axis_size(axis) for axis in ("lat", "lon", "dp"))
    cap = obs_vectors.shape[0] * 3 // (2 * n_lat)
    fits = (
        n_dp == 2
        and n_lon > 2
        and n_lon & (n_lon - 1) == 0
        and n_lat * TILE <= LANES
        and n_lat <= TILE
        and cap * 2 == TILE * 3
        and lat_dev == WIN
        and lon_dev == 2 * WIN
        and d_model // n_lon % LANES == 0
        and d_model // (n_lat * n_dp) == LANES
        and d_model // HEADS * 2 == LANES
    )
    program = fast_program if fits else general_program
    return program(tokens, norm_gain, w_qkv, w_out, obs_vectors, *rest)


def solution(mesh):
    placed = (
        P("dp", None, "lat", "lon", None),
        P(),
        P(),
        P(),
        P(("lon", "lat", "dp"), None),
        P(("lon", "lat", "dp"), None),
        P(("lon", "lat", "dp")),
        P(("lon", "lat", "dp")),
        P("dp", None),
        P("dp", None, "lat", "lon", None),
    )
    return jax.shard_map(
        on_device,
        mesh=mesh,
        in_specs=placed,
        out_specs=(P("dp", None, "lat", "lon", None), P("lon", ("lat", "dp"))),
        check_vma=False,
    )
```

```python
import functools

import jax
import jax.numpy as jnp
from jax import lax
from jax.experimental import pallas as pl
from jax.experimental.pallas import tpu as pltpu
from jax.sharding import PartitionSpec as P

HEADS = 16
WIN = 8
BF16 = jnp.bfloat16
F32 = jnp.float32
LANES = 128
TILE = 16
VMEM_LIMIT = 24 * 1024 * 1024
SLOW = 10**10


def from_behind(array, axis, by):
    devices = lax.axis_size(axis)
    pairs = [(i, i + by) for i in range(devices) if 0 <= i + by < devices]
    return lax.ppermute(array, axis, pairs)


def shifted(array, axis, by):
    devices = lax.axis_size(axis)
    return lax.ppermute(array, axis, [(i, (i + by) % devices) for i in range(devices)])


def swapped(array, axis, bit):
    devices = lax.axis_size(axis)
    return lax.ppermute(array, axis, [(i, i ^ bit) for i in range(devices)])


def to_windows(field_in):
    levels_n, rows_n, cols_n, feat_width = field_in.shape
    blocks = field_in.reshape(levels_n, rows_n // WIN, WIN, cols_n // WIN, WIN, feat_width)
    return blocks.transpose(1, 3, 0, 2, 4, 5).reshape(-1, levels_n * WIN * WIN, feat_width)


def from_windows(windows, levels_n, rows_n, cols_n):
    feat_width = windows.shape[-1]
    blocks = windows.reshape(rows_n // WIN, cols_n // WIN, levels_n, WIN, WIN, feat_width)
    return blocks.transpose(2, 0, 3, 1, 4, 5).reshape(levels_n, rows_n, cols_n, feat_width)


def window_block(win_tokens, win_valid, norm_gain, w_qkv, w_out):
    n_win, n_tok, d_model = win_tokens.shape
    head_dim = d_model // HEADS
    as_float = win_tokens.astype(F32)
    average = jnp.mean(as_float, axis=-1, keepdims=True)
    centred = as_float - average
    variance = jnp.mean(centred * centred, axis=-1, keepdims=True)
    normed = (centred * lax.rsqrt(variance + 1e-05) * norm_gain).astype(BF16)
    projected = jnp.dot(
        normed.reshape(-1, d_model), w_qkv, preferred_element_type=F32
    ).astype(BF16)
    projected = projected.reshape(n_win, n_tok, 3, HEADS, head_dim)
    queries = projected[:, :, 0]
    key_rows = projected[:, :, 1]
    values = projected[:, :, 2]
    scores = jnp.einsum(
        "wqhd,wkhd->whqk", queries, key_rows, preferred_element_type=F32
    ) * head_dim ** (-0.5)
    scores = jnp.where(win_valid[:, None, None, :], scores, -1e30)
    highest = jnp.max(scores, axis=-1, keepdims=True)
    powers = jnp.exp(scores - highest)
    weights = (powers / jnp.sum(powers, axis=-1, keepdims=True)).astype(BF16)
    context = jnp.einsum(
        "whqk,wkhd->wqhd", weights, values, preferred_element_type=F32
    ).astype(BF16)
    context = context.reshape(n_win, n_tok, d_model)
    result = jnp.dot(context.reshape(-1, d_model), w_out, preferred_element_type=F32)
    return ((as_float + result.reshape(n_win, n_tok, d_model)).astype(BF16), context)


def general_program(
    tokens, norm_gain, w_qkv, w_out, obs_vectors, obs_lat, obs_cell, obs_count, shift_offsets, cotangent
):
    n_batch, levels, lat_dev, lon_dev, d_model = tokens.shape
    n_lat = lax.axis_size("lat")
    obs_rows = obs_vectors.shape[0]
    capacity = obs_rows * 3 // (2 * n_lat)
    n_slots = n_lat * capacity
    destination = obs_lat[:, 0]
    one_hot = (destination[:, None] == jnp.arange(n_lat, dtype=jnp.int32)[None, :]).astype(jnp.int32)
    earlier = jnp.cumsum(one_hot, axis=0) - one_hot
    rank_in = jnp.sum(earlier * one_hot, axis=1)
    slot_of = destination * capacity + rank_in
    is_live = jnp.arange(obs_rows, dtype=jnp.int32) < obs_count[0]
    cell_tag = jnp.where(is_live, obs_cell, -1)
    chooser = slot_of[None, :] == jnp.arange(n_slots, dtype=jnp.int32)[:, None]
    sent_rows = (
        jnp.dot(chooser.astype(BF16), obs_vectors, preferred_element_type=F32)
        .astype(BF16)
        .reshape(n_lat, capacity, d_model)
    )
    sent_tags = (jnp.sum(chooser.astype(jnp.int32) * (cell_tag[None, :] + 1), axis=1) - 1).reshape(
        n_lat, capacity
    )
    got_rows, got_tags = (
        lax.all_to_all(sent_rows, "lat", split_axis=0, concat_axis=0, tiled=True),
        lax.all_to_all(sent_tags, "lat", split_axis=0, concat_axis=0, tiled=True),
    )
    flat_tokens = tokens.reshape(-1, d_model)
    placer = (
        got_tags.reshape(-1)[None, :] == jnp.arange(flat_tokens.shape[0], dtype=jnp.int32)[:, None]
    ).astype(BF16)
    added = jnp.dot(placer, got_rows.reshape(-1, d_model), preferred_element_type=F32)
    enriched = (flat_tokens.astype(F32) + added).astype(BF16).reshape(tokens.shape)
    margin = WIN - 1
    north_part = from_behind(enriched[:, :, :margin], "lat", -1)
    heightened = jnp.concatenate([enriched, north_part], axis=2)
    east_cols = shifted(heightened[:, :, :, :margin], "lon", -1)
    extended = jnp.concatenate([heightened, east_cols], axis=3)
    lat_shift = shift_offsets[0, 0]
    lon_shift = shift_offsets[0, 1]
    anchor = jnp.zeros((), jnp.int32)
    region = lax.dynamic_slice(
        extended, (anchor, anchor, lat_shift, lon_shift, anchor), tokens.shape
    )[0]
    source_rows = lax.axis_index("lat") * lat_dev + lat_shift + jnp.arange(lat_dev, dtype=jnp.int32)
    is_valid = jnp.broadcast_to(
        (source_rows < lat_dev * n_lat)[None, :, None, None], (levels, lat_dev, lon_dev, 1)
    )
    mixed, context = window_block(
        to_windows(region), to_windows(is_valid)[..., 0], norm_gain, w_qkv, w_out
    )
    block_out = from_windows(mixed, levels, lat_dev, lon_dev)[None]
    cot_rows = to_windows(cotangent[0]).reshape(-1, d_model)
    context_rows = context.reshape(-1, d_model)
    contract = (((0,), (0,)), ((), ()))
    partial_rows = lax.psum_scatter(
        lax.dot_general(cot_rows, context_rows, contract, preferred_element_type=F32),
        "lon",
        scatter_dimension=0,
        tiled=True,
    )
    gradient = lax.psum_scatter(partial_rows, ("lat", "dp"), scatter_dimension=1, tiled=True)
    return (block_out, gradient)


def call(body, out_shape, args, specs, name, scratch=(), flops=1, moved=1):
    return pl.pallas_call(
        body,
        out_shape=out_shape,
        in_specs=specs,
        out_specs=jax.tree.map(lambda _: pl.BlockSpec(memory_space=pltpu.VMEM), out_shape),
        scratch_shapes=list(scratch),
        compiler_params=pltpu.CompilerParams(vmem_limit_bytes=VMEM_LIMIT),
        cost_estimate=pl.CostEstimate(flops=flops, bytes_accessed=moved, transcendentals=0),
        name=name,
    )(*args)


VMEM_SPEC = pl.BlockSpec(memory_space=pltpu.VMEM)
SMEM_SPEC = pl.BlockSpec(memory_space=pltpu.SMEM)
ANY_SPEC = pl.BlockSpec(memory_space=pl.ANY)


def iota(shape, dim):
    return lax.broadcasted_iota(jnp.int32, shape, dim)


def matmul(lhs, rhs):
    return jnp.dot(lhs, rhs, preferred_element_type=F32)


def copy_all(pairs, sems):
    copies = [pltpu.make_async_copy(src, dst, sems.at[i]) for i, (src, dst) in enumerate(pairs)]
    for copy in copies:
        copy.start()
    return copies


def above_body(above_ref):
    above_ref[...] = (iota(above_ref.shape, 0) < iota(above_ref.shape, 1)).astype(BF16)


def live_body(count_ref, live_ref):
    live_ref[...] = (iota(live_ref.shape, 1) < count_ref[0]).astype(jnp.int32)


def route_body(n_lat, above_ref, live_ref, cell_ref, lat_ref, vec_ref, *out_refs):
    rows = vec_ref.shape[0]
    here = lax.axis_index("lat")
    slot = iota((LANES, rows), 0)
    tag = (live_ref[...] * (cell_ref[...] + 1)).astype(F32)
    lat = lat_ref[...]
    named = (iota((TILE, rows), 0) == lat).astype(BF16)
    rank = jnp.sum(matmul(named, above_ref[...]) * named.astype(F32), axis=0, keepdims=True)
    rank = rank.astype(jnp.int32)
    base = jnp.where(lat < here, lat - here + n_lat, lat - here) * TILE
    late = rank >= TILE
    choosers = [
        (slot == jnp.where(chosen, base + rank - back, -1)).astype(BF16)
        for chosen, back in ((rank < TILE, 0), (late, TILE), (late, TILE // 2))
    ]
    tags = sum(
        lax.dot_general(
            jnp.where(slot == base + i, tag, 0.0).astype(BF16),
            chooser,
            (((1,), (1,)), ((), ())),
            preferred_element_type=F32,
        )
        for i, chooser in enumerate(choosers)
    )
    width = vec_ref.shape[1]
    picked = matmul(choosers[0], vec_ref[...])
    extra = matmul(choosers[1], vec_ref[:, : width // 2])
    extra = extra + matmul(choosers[2], vec_ref[:, width // 2 :])
    for k, out_ref in enumerate(out_refs):
        piece = slice(k * TILE, (k + 1) * TILE)
        out_ref[:, :width] = picked[piece].astype(BF16)
        out_ref[:, width : width + width // 2] = extra[piece].astype(BF16)
        out_ref[:, width + width // 2 :] = tags[piece].astype(BF16)


def load_body(*refs):
    count = len(refs) // 2
    for copy in copy_all(list(zip(refs[:count], refs[count:-1])), refs[-1]):
        copy.wait()


def load(arrays, name):
    return call(
        load_body,
        [jax.ShapeDtypeStruct(array.shape, array.dtype) for array in arrays],
        tuple(in_hbm(array) for array in arrays),
        [ANY_SPEC] * len(arrays),
        name,
        [pltpu.SemaphoreType.DMA((len(arrays),))],
    )


def weights_body(groups, n_lat, n_dp, *refs):
    (wqkv_hbm, wqkv_ref), sems = refs[0::3][:2], refs[-1]
    width = wqkv_hbm.shape[0]
    d_blk = width // (n_lat * n_dp)
    pairs = [(refs[2], refs[5]), (refs[1], refs[4])]
    to = 0
    for part, turns in groups:
        for third in range(3):
            for k in turns:
                at = pl.multiple_of(third * width + block_start(part, k, n_lat, n_dp, d_blk), d_blk)
                pairs.append((wqkv_hbm.at[:, pl.ds(at, d_blk)], wqkv_ref.at[:, to : to + d_blk]))
                to += d_blk
    for copy in copy_all(pairs, sems):
        copy.wait()


def stage_body(sizes, shift_ref, tok_hbm, tok_ref, pick_ref, sem):
    copy = pltpu.make_async_copy(tok_hbm, tok_ref, sem)
    copy.start()
    lat_shift, lon_shift = shift_ref[:, :1], shift_ref[:, 1:]
    n_rows, n_cols = pick_ref.shape
    n_tok = n_rows // 2
    row = iota((n_rows, 1), 0)
    level = row // (WIN * WIN) % (n_tok // (WIN * WIN))
    at_lat = row // WIN % WIN + lat_shift
    at_lon = row % WIN + row // n_tok * WIN + lon_shift
    cols, margin = 2 * WIN, WIN - 1
    starts = [sum(sizes[:i]) for i in range(len(sizes))]
    inside = (level * WIN + at_lat) * cols + at_lon
    north = (level * margin + at_lat - WIN) * WIN + at_lon % WIN
    east = (level * WIN + at_lat) * WIN + at_lon - cols
    index = jnp.where(
        at_lat < WIN,
        jnp.where(at_lon < cols, inside, east + starts[3]),
        north + jnp.where(at_lon < WIN, starts[1], jnp.where(at_lon < cols, starts[2], starts[4])),
    )
    pick_ref[...] = (index == iota((n_rows, n_cols), 1)).astype(BF16)
    copy.wait()


def enrich_body(n_lat, tok_ref, *refs):
    parts, (own_ref, north0_ref, north1_ref, east_ref) = refs[:n_lat], refs[n_lat:]
    _, levels, rows, cols, width = tok_ref.shape
    n_tok = levels * rows * cols
    half = width // 2
    tags = sum(part[:, width + half :].astype(F32) for part in parts).astype(jnp.int32)
    row = iota((n_tok, LANES), 0) + 1
    places = [(tags[i : i + 1] == row).astype(BF16)[:, : n_lat * TILE] for i in range(3)]
    got = jnp.concatenate([part[...] for part in parts], axis=0)
    extra = got[:, width : width + half]
    total = tok_ref[...].reshape(n_tok, width).astype(F32) + matmul(places[0], got[:, :width])
    total = total + jnp.concatenate([matmul(place, extra) for place in places[1:]], axis=1)
    own_ref[...] = total.astype(BF16)
    grid = total.reshape(levels, rows, cols, width)
    for out_ref, part in (
        (north0_ref, grid[:, : rows - 1, :WIN]),
        (north1_ref, grid[:, : rows - 1, WIN:]),
        (east_ref, grid[:, :, :WIN]),
    ):
        out_ref[...] = part.reshape(out_ref.shape).astype(BF16)


def region_body(pick_ref, gain_ref, *refs):
    sources, (region_ref, normed_ref) = refs[:-2], refs[-2:]
    region = matmul(pick_ref[...], jnp.concatenate([ref[...] for ref in sources], axis=0))
    region_ref[...] = region.astype(BF16)
    centred = region - jnp.mean(region, axis=-1, keepdims=True)
    variance = jnp.mean(centred * centred, axis=-1, keepdims=True)
    normed_ref[...] = (centred * lax.rsqrt(variance + 1e-05) * gain_ref[...]).astype(BF16)


def block_start(part, k, n_lat, n_dp, d_blk):
    lat = lax.axis_index("lat") + k
    lat = jnp.where(lat >= n_lat, lat - n_lat, lat)
    dp = lax.axis_index("dp")
    dp = 1 - dp if part else dp
    return pl.multiple_of((lat * n_dp + dp) * d_blk, d_blk)


def attend_body(group, turns, n_lat, n_dp, normed_ref, wqkv_ref, shift_ref, out_ref):
    n_rows, width = normed_ref.shape
    n_tok = n_rows // 2
    d_blk = width // (n_lat * n_dp)
    part = len(turns) * d_blk
    at = 3 * group * part
    every = matmul(normed_ref[...], wqkv_ref[:, at : at + 3 * part])
    thirds = [every[:, i * part : (i + 1) * part] for i in range(3)]
    scale = (d_blk // 2) ** (-0.5)
    queries = (thirds[0].astype(BF16).astype(F32) * scale).astype(BF16)
    keys, values = thirds[1].astype(BF16), thirds[2].astype(BF16)
    key = iota((1, n_tok), 1)
    valid = lax.axis_index("lat") * WIN + key // WIN % WIN + shift_ref[:, :1] < WIN * n_lat
    first = iota((n_tok, d_blk), 1) < d_blk // 2
    ones, none = jnp.ones((n_tok, d_blk), BF16), jnp.zeros((n_tok, d_blk), BF16)
    units = [
        (slice(which * n_tok, (which + 1) * n_tok), slice(k * d_blk, (k + 1) * d_blk))
        for which in range(2)
        for k in range(len(turns))
    ]
    scores = []
    for unit in units:
        query = queries[unit]
        both = jnp.concatenate(
            [jnp.where(first, query, none), jnp.where(first, none, query)], axis=0
        )
        scores.append(
            lax.dot_general(both, keys[unit], (((1,), (1,)), ((), ())), preferred_element_type=F32)
        )
    scores = [jnp.where(valid, score, -1e30) for score in scores]
    highest = [jnp.max(score, axis=-1, keepdims=True) for score in scores]
    powers = [jnp.exp(score - top).astype(BF16) for score, top in zip(scores, highest)]
    mixed = [
        matmul(power, jnp.concatenate([values[unit], ones], axis=1))
        for power, unit in zip(powers, units)
    ]
    for context, unit in zip(mixed, units):
        context = context[:, :d_blk] / context[:, d_blk:]
        out_ref[unit] = jnp.where(first, context[:n_tok], context[n_tok:]).astype(BF16)


def turn_body(n_lon, cot_ref, other_ref, out_ref, flat_ref):
    _, levels, rows, cols, width = cot_ref.shape
    e_blk = width // n_lon
    n_tok = levels * rows * WIN
    here = lax.axis_index("lon")
    at = 0
    for ref in (cot_ref, other_ref):
        grid = ref[...].astype(F32).reshape(levels * rows, cols, width)
        for which in range(cols // WIN):
            flat_ref[...] = grid[:, which * WIN : (which + 1) * WIN].reshape(n_tok, width)
            for place, block in enumerate(reversed_order(n_lon)):
                lon = here ^ block
                piece = flat_ref[:, pl.ds(pl.multiple_of(lon * e_blk, e_blk), e_blk)]
                out_ref[place, :, at : at + n_tok] = piece.T.astype(BF16)
            at += n_tok


def reversed_order(count):
    bits = count.bit_length() - 1
    return [int(format(i, f"0{bits}b")[::-1], 2) if bits else 0 for i in range(count)]


def project_body(groups, n_lat, n_dp, reg_ref, wout_ref, *refs):
    ctx_refs, out_ref = refs[:-1], refs[-1]
    _, levels, rows, cols, width = out_ref.shape
    d_blk = width // (n_lat * n_dp)
    mixed = reg_ref[...].astype(F32)
    for (part, turns), ctx_ref in zip(groups, ctx_refs):
        starts = [block_start(part, k, n_lat, n_dp, d_blk) for k in turns]
        weights = jnp.concatenate([wout_ref[pl.ds(at, d_blk), :] for at in starts], axis=0)
        mixed = mixed + matmul(ctx_ref[...], weights)
    n_tok = levels * rows * WIN
    halves = [
        mixed[i * n_tok : (i + 1) * n_tok].reshape(levels * rows, WIN, width)
        for i in range(cols // WIN)
    ]
    out_ref[...] = jnp.concatenate(halves, axis=1).astype(BF16).reshape(out_ref.shape)


def gradient_body(cot_ref, mine_ref, other_ref, keep_ref, send_ref):
    context = jnp.concatenate([mine_ref[...], other_ref[...]], axis=0)
    count = cot_ref.shape[0] // 2
    for place in range(count):
        send_ref[place] = matmul(cot_ref[count + place], context).astype(BF16)
    for place in range(count):
        keep_ref[place] = matmul(cot_ref[place], context)


def in_hbm(array):
    return pltpu.with_memory_space_constraint(array, pltpu.HBM)


def fast_program(
    tokens, norm_gain, w_qkv, w_out, obs_vectors, obs_lat, obs_cell, obs_count, shift_offsets, cotangent
):
    _, levels, lat_dev, lon_dev, d_model = tokens.shape
    n_lat, n_lon, n_dp = (lax.axis_size(axis) for axis in ("lat", "lon", "dp"))
    shape = jax.ShapeDtypeStruct
    n_tok = levels * lat_dev * WIN
    n_rows = levels * lat_dev * lon_dev
    n_margin = levels * (lat_dev - 1) * WIN
    e_blk = d_model // n_lon
    d_blk = d_model // (n_lat * n_dp)
    dma = pltpu.SemaphoreType.DMA

    fetched = (obs_cell.reshape(1, -1), obs_lat.reshape(1, -1), obs_vectors)
    obs_rows = obs_vectors.shape[0]
    above = call(above_body, shape((obs_rows, obs_rows), BF16), (), [], "above", flops=SLOW)
    above, obs_count = lax.optimization_barrier((above, obs_count))
    live = call(
        live_body,
        shape(fetched[0].shape, jnp.int32),
        (obs_count,),
        [SMEM_SPEC],
        "live",
    )
    payload = call(
        functools.partial(route_body, n_lat),
        [shape((TILE, d_model + d_model // 2 + LANES), BF16)] * n_lat,
        (above, live, *fetched),
        [VMEM_SPEC] * 5,
        "route",
    )
    arrived = [payload[0]] + [shifted(payload[k], "lat", k) for k in range(1, n_lat)]

    sizes = (n_rows, n_margin, n_margin, n_tok, n_margin)
    shift_offsets, tokens = lax.optimization_barrier((payload[0], shift_offsets, tokens))[1:]
    tokens, picks = call(
        functools.partial(stage_body, sizes),
        [shape(tokens.shape, BF16), shape((n_rows, sum(sizes)), BF16)],
        (shift_offsets, in_hbm(tokens)),
        [VMEM_SPEC, ANY_SPEC],
        "stage",
        [dma],
    )
    own, north0, north1, east = call(
        functools.partial(enrich_body, n_lat),
        [shape((n, d_model), BF16) for n in (n_rows, n_margin, n_margin, n_tok)],
        (tokens, *arrived),
        [VMEM_SPEC] * (1 + n_lat),
        "enrich",
    )
    north0 = from_behind(north0, "lat", -1)
    north1 = from_behind(north1, "lat", -1)
    east = shifted(east, "lon", -1)
    cot_other = swapped(cotangent, "dp", 1)
    corner = shifted(north0, "lon", -1)
    loaded = (w_qkv, w_out, norm_gain.reshape(1, -1))
    loaded = lax.optimization_barrier((north0, *loaded))[1:]
    first, second = [k for k in range(n_lat) if k % 3], [k for k in range(n_lat) if k % 3 == 0]
    groups = [(1, first), (0, first), (1, second), (0, second)]
    w_qkv, w_out, gain = call(
        functools.partial(weights_body, groups, n_lat, n_dp),
        [shape(array.shape, array.dtype) for array in loaded],
        tuple(in_hbm(array) for array in loaded),
        [ANY_SPEC] * 3,
        "weights",
        [dma((2 + 3 * n_lat * n_dp,))],
    )
    region, normed = call(
        region_body,
        [shape((n_rows, d_model), BF16)] * 2,
        (picks, gain, own, north0, north1, east, corner),
        [VMEM_SPEC] * 7,
        "region",
    )
    first, second = [k for k in range(n_lat) if k % 3], [k for k in range(n_lat) if k % 3 == 0]

    def attend(normed, part, turns):
        return call(
            functools.partial(attend_body, groups.index((part, turns)), turns, n_lat, n_dp),
            shape((n_rows, len(turns) * d_blk), BF16),
            (normed, w_qkv, shift_offsets),
            [VMEM_SPEC] * 3,
            f"attend{part}{turns[0]}",
            flops=SLOW if (part, turns) == (0, second) else 1,
        )

    def local_gradient(turns, mine, other, cost):
        width = len(turns) * d_blk
        return call(
            gradient_body,
            [shape((n_lon // 2, e_blk, width), F32), shape((n_lon // 2, e_blk, width), BF16)],
            (cot_turned, mine, other),
            [VMEM_SPEC] * 3,
            f"gradient{turns[0]}",
            flops=cost,
        )

    def halves(total):
        middle = total.shape[0] // 2
        return total[:middle], total[middle:].astype(BF16)

    def fold(kept, sent, bit):
        return kept + swapped(sent, "lon", bit).astype(F32)

    def over_lon(total, bit):
        while bit < n_lon:
            total = fold(*halves(total), bit)
            bit *= 2
        return total

    def over_lat(total, turns):
        blocks = []
        for i, k in enumerate(turns):
            block = total[..., i * d_blk : (i + 1) * d_blk]
            blocks.append(shifted(block.astype(BF16), "lat", k).astype(F32) if k else block)
        return functools.reduce(jnp.add, blocks)

    def after(array, *others):
        return lax.optimization_barrier((array, *others))[0]

    cot_turned = call(
        functools.partial(turn_body, n_lon),
        shape((n_lon, e_blk, n_dp * n_rows), BF16),
        (cotangent, cot_other),
        [VMEM_SPEC] * 2,
        "turn",
        [pltpu.VMEM((n_tok, d_model), F32)],
    )
    theirs0 = attend(normed, 1, first)
    got0 = swapped(theirs0, "dp", 1)
    mine0 = attend(after(normed, theirs0), 0, first)
    theirs1 = attend(after(normed, mine0), 1, second)
    got1 = swapped(theirs1, "dp", 1)
    kept0, sent0 = local_gradient(first, mine0, after(got0, theirs1), 1)
    mine1 = attend(after(normed, sent0), 0, second)
    kept0, sent0 = halves(fold(after(kept0, mine1), sent0, 1))
    kept1, sent1 = local_gradient(second, mine1, after(got1, sent0), SLOW)
    kept1, sent1 = halves(fold(kept1, sent1, 1))
    groups = [(1, first), (0, first), (1, second), (0, second)]
    block_out = call(
        functools.partial(project_body, groups, n_lat, n_dp),
        shape((1, levels, lat_dev, lon_dev, d_model), BF16),
        (after(region, sent0), w_out, theirs0, mine0, theirs1, mine1),
        [VMEM_SPEC] * 6,
        "project",
        flops=SLOW,
    )
    total0 = fold(after(kept0, block_out, sent1), sent0, 2)
    total1 = fold(kept1, sent1, 2)
    gradient = over_lat(over_lon(total0, 4), first)
    gradient, total1 = lax.optimization_barrier((gradient, over_lat(over_lon(total1, 4), second)))
    gradient = (gradient + total1)[0]
    return (block_out, gradient)


def on_device(tokens, norm_gain, w_qkv, w_out, obs_vectors, *rest):
    _, _, lat_dev, lon_dev, d_model = tokens.shape
    n_lat, n_lon, n_dp = (lax.axis_size(axis) for axis in ("lat", "lon", "dp"))
    cap = obs_vectors.shape[0] * 3 // (2 * n_lat)
    fits = (
        n_dp == 2
        and n_lon > 2
        and n_lon & (n_lon - 1) == 0
        and n_lat * TILE <= LANES
        and n_lat <= TILE
        and cap * 2 == TILE * 3
        and lat_dev == WIN
        and lon_dev == 2 * WIN
        and d_model // n_lon % LANES == 0
        and d_model // (n_lat * n_dp) == LANES
        and d_model // HEADS * 2 == LANES
    )
    program = fast_program if fits else general_program
    return program(tokens, norm_gain, w_qkv, w_out, obs_vectors, *rest)


def solution(mesh):
    placed = (
        P("dp", None, "lat", "lon", None),
        P(),
        P(),
        P(),
        P(("lon", "lat", "dp"), None),
        P(("lon", "lat", "dp"), None),
        P(("lon", "lat", "dp")),
        P(("lon", "lat", "dp")),
        P("dp", None),
        P("dp", None, "lat", "lon", None),
    )
    return jax.shard_map(
        on_device,
        mesh=mesh,
        in_specs=placed,
        out_specs=(P("dp", None, "lat", "lon", None), P("lon", ("lat", "dp"))),
        check_vma=False,
    )
```

```python
import functools

import jax
import jax.numpy as jnp
from jax import lax
from jax.experimental import pallas as pl
from jax.experimental.pallas import tpu as pltpu
from jax.sharding import PartitionSpec as P

HEADS = 16
WIN = 8
BF16 = jnp.bfloat16
F32 = jnp.float32
LANES = 128
TILE = 16
VMEM_LIMIT = 24 * 1024 * 1024
SLOW = 10**10


def from_behind(array, axis, by):
    devices = lax.axis_size(axis)
    pairs = [(i, i + by) for i in range(devices) if 0 <= i + by < devices]
    return lax.ppermute(array, axis, pairs)


def shifted(array, axis, by):
    devices = lax.axis_size(axis)
    return lax.ppermute(array, axis, [(i, (i + by) % devices) for i in range(devices)])


def swapped(array, axis, bit):
    devices = lax.axis_size(axis)
    return lax.ppermute(array, axis, [(i, i ^ bit) for i in range(devices)])


def to_windows(field_in):
    levels_n, rows_n, cols_n, feat_width = field_in.shape
    blocks = field_in.reshape(levels_n, rows_n // WIN, WIN, cols_n // WIN, WIN, feat_width)
    return blocks.transpose(1, 3, 0, 2, 4, 5).reshape(-1, levels_n * WIN * WIN, feat_width)


def from_windows(windows, levels_n, rows_n, cols_n):
    feat_width = windows.shape[-1]
    blocks = windows.reshape(rows_n // WIN, cols_n // WIN, levels_n, WIN, WIN, feat_width)
    return blocks.transpose(2, 0, 3, 1, 4, 5).reshape(levels_n, rows_n, cols_n, feat_width)


def window_block(win_tokens, win_valid, norm_gain, w_qkv, w_out):
    n_win, n_tok, d_model = win_tokens.shape
    head_dim = d_model // HEADS
    as_float = win_tokens.astype(F32)
    average = jnp.mean(as_float, axis=-1, keepdims=True)
    centred = as_float - average
    variance = jnp.mean(centred * centred, axis=-1, keepdims=True)
    normed = (centred * lax.rsqrt(variance + 1e-05) * norm_gain).astype(BF16)
    projected = jnp.dot(
        normed.reshape(-1, d_model), w_qkv, preferred_element_type=F32
    ).astype(BF16)
    projected = projected.reshape(n_win, n_tok, 3, HEADS, head_dim)
    queries = projected[:, :, 0]
    key_rows = projected[:, :, 1]
    values = projected[:, :, 2]
    scores = jnp.einsum(
        "wqhd,wkhd->whqk", queries, key_rows, preferred_element_type=F32
    ) * head_dim ** (-0.5)
    scores = jnp.where(win_valid[:, None, None, :], scores, -1e30)
    highest = jnp.max(scores, axis=-1, keepdims=True)
    powers = jnp.exp(scores - highest)
    weights = (powers / jnp.sum(powers, axis=-1, keepdims=True)).astype(BF16)
    context = jnp.einsum(
        "whqk,wkhd->wqhd", weights, values, preferred_element_type=F32
    ).astype(BF16)
    context = context.reshape(n_win, n_tok, d_model)
    result = jnp.dot(context.reshape(-1, d_model), w_out, preferred_element_type=F32)
    return ((as_float + result.reshape(n_win, n_tok, d_model)).astype(BF16), context)


def general_program(
    tokens, norm_gain, w_qkv, w_out, obs_vectors, obs_lat, obs_cell, obs_count, shift_offsets, cotangent
):
    n_batch, levels, lat_dev, lon_dev, d_model = tokens.shape
    n_lat = lax.axis_size("lat")
    obs_rows = obs_vectors.shape[0]
    capacity = obs_rows * 3 // (2 * n_lat)
    n_slots = n_lat * capacity
    destination = obs_lat[:, 0]
    one_hot = (destination[:, None] == jnp.arange(n_lat, dtype=jnp.int32)[None, :]).astype(jnp.int32)
    earlier = jnp.cumsum(one_hot, axis=0) - one_hot
    rank_in = jnp.sum(earlier * one_hot, axis=1)
    slot_of = destination * capacity + rank_in
    is_live = jnp.arange(obs_rows, dtype=jnp.int32) < obs_count[0]
    cell_tag = jnp.where(is_live, obs_cell, -1)
    chooser = slot_of[None, :] == jnp.arange(n_slots, dtype=jnp.int32)[:, None]
    sent_rows = (
        jnp.dot(chooser.astype(BF16), obs_vectors, preferred_element_type=F32)
        .astype(BF16)
        .reshape(n_lat, capacity, d_model)
    )
    sent_tags = (jnp.sum(chooser.astype(jnp.int32) * (cell_tag[None, :] + 1), axis=1) - 1).reshape(
        n_lat, capacity
    )
    got_rows, got_tags = (
        lax.all_to_all(sent_rows, "lat", split_axis=0, concat_axis=0, tiled=True),
        lax.all_to_all(sent_tags, "lat", split_axis=0, concat_axis=0, tiled=True),
    )
    flat_tokens = tokens.reshape(-1, d_model)
    placer = (
        got_tags.reshape(-1)[None, :] == jnp.arange(flat_tokens.shape[0], dtype=jnp.int32)[:, None]
    ).astype(BF16)
    added = jnp.dot(placer, got_rows.reshape(-1, d_model), preferred_element_type=F32)
    enriched = (flat_tokens.astype(F32) + added).astype(BF16).reshape(tokens.shape)
    margin = WIN - 1
    north_part = from_behind(enriched[:, :, :margin], "lat", -1)
    heightened = jnp.concatenate([enriched, north_part], axis=2)
    east_cols = shifted(heightened[:, :, :, :margin], "lon", -1)
    extended = jnp.concatenate([heightened, east_cols], axis=3)
    lat_shift = shift_offsets[0, 0]
    lon_shift = shift_offsets[0, 1]
    anchor = jnp.zeros((), jnp.int32)
    region = lax.dynamic_slice(
        extended, (anchor, anchor, lat_shift, lon_shift, anchor), tokens.shape
    )[0]
    source_rows = lax.axis_index("lat") * lat_dev + lat_shift + jnp.arange(lat_dev, dtype=jnp.int32)
    is_valid = jnp.broadcast_to(
        (source_rows < lat_dev * n_lat)[None, :, None, None], (levels, lat_dev, lon_dev, 1)
    )
    mixed, context = window_block(
        to_windows(region), to_windows(is_valid)[..., 0], norm_gain, w_qkv, w_out
    )
    block_out = from_windows(mixed, levels, lat_dev, lon_dev)[None]
    cot_rows = to_windows(cotangent[0]).reshape(-1, d_model)
    context_rows = context.reshape(-1, d_model)
    contract = (((0,), (0,)), ((), ()))
    partial_rows = lax.psum_scatter(
        lax.dot_general(cot_rows, context_rows, contract, preferred_element_type=F32),
        "lon",
        scatter_dimension=0,
        tiled=True,
    )
    gradient = lax.psum_scatter(partial_rows, ("lat", "dp"), scatter_dimension=1, tiled=True)
    return (block_out, gradient)


def call(body, out_shape, args, specs, name, scratch=(), flops=1, moved=1):
    return pl.pallas_call(
        body,
        out_shape=out_shape,
        in_specs=specs,
        out_specs=jax.tree.map(lambda _: pl.BlockSpec(memory_space=pltpu.VMEM), out_shape),
        scratch_shapes=list(scratch),
        compiler_params=pltpu.CompilerParams(vmem_limit_bytes=VMEM_LIMIT),
        cost_estimate=pl.CostEstimate(flops=flops, bytes_accessed=moved, transcendentals=0),
        name=name,
    )(*args)


VMEM_SPEC = pl.BlockSpec(memory_space=pltpu.VMEM)
SMEM_SPEC = pl.BlockSpec(memory_space=pltpu.SMEM)
ANY_SPEC = pl.BlockSpec(memory_space=pl.ANY)


def iota(shape, dim):
    return lax.broadcasted_iota(jnp.int32, shape, dim)


def matmul(lhs, rhs):
    return jnp.dot(lhs, rhs, preferred_element_type=F32)


def copy_all(pairs, sems):
    copies = [pltpu.make_async_copy(src, dst, sems.at[i]) for i, (src, dst) in enumerate(pairs)]
    for copy in copies:
        copy.start()
    return copies


def above_body(above_ref):
    above_ref[...] = (iota(above_ref.shape, 0) < iota(above_ref.shape, 1)).astype(BF16)


def live_body(count_ref, live_ref):
    live_ref[...] = (iota(live_ref.shape, 1) < count_ref[0]).astype(jnp.int32)


def route_body(n_lat, above_ref, live_ref, cell_ref, lat_ref, vec_ref, *out_refs):
    rows = vec_ref.shape[0]
    here = lax.axis_index("lat")
    slot = iota((LANES, rows), 0)
    tag = (live_ref[...] * (cell_ref[...] + 1)).astype(F32)
    lat = lat_ref[...]
    named = (iota((TILE, rows), 0) == lat).astype(BF16)
    rank = jnp.sum(matmul(named, above_ref[...]) * named.astype(F32), axis=0, keepdims=True)
    rank = rank.astype(jnp.int32)
    base = jnp.where(lat < here, lat - here + n_lat, lat - here) * TILE
    late = rank >= TILE
    choosers = [
        (slot == jnp.where(chosen, base + rank - back, -1)).astype(BF16)
        for chosen, back in ((rank < TILE, 0), (late, TILE), (late, TILE // 2))
    ]
    tags = sum(
        lax.dot_general(
            jnp.where(slot == base + i, tag, 0.0).astype(BF16),
            chooser,
            (((1,), (1,)), ((), ())),
            preferred_element_type=F32,
        )
        for i, chooser in enumerate(choosers)
    )
    width = vec_ref.shape[1]
    picked = matmul(choosers[0], vec_ref[...])
    extra = matmul(choosers[1], vec_ref[:, : width // 2])
    extra = extra + matmul(choosers[2], vec_ref[:, width // 2 :])
    for k, out_ref in enumerate(out_refs):
        piece = slice(k * TILE, (k + 1) * TILE)
        out_ref[:, :width] = picked[piece].astype(BF16)
        out_ref[:, width : width + width // 2] = extra[piece].astype(BF16)
        out_ref[:, width + width // 2 :] = tags[piece].astype(BF16)


def load_body(*refs):
    count = len(refs) // 2
    for copy in copy_all(list(zip(refs[:count], refs[count:-1])), refs[-1]):
        copy.wait()


def load(arrays, name):
    return call(
        load_body,
        [jax.ShapeDtypeStruct(array.shape, array.dtype) for array in arrays],
        tuple(in_hbm(array) for array in arrays),
        [ANY_SPEC] * len(arrays),
        name,
        [pltpu.SemaphoreType.DMA((len(arrays),))],
    )


def stage_body(sizes, shift_ref, tok_hbm, tok_ref, pick_ref, sem):
    copy = pltpu.make_async_copy(tok_hbm, tok_ref, sem)
    copy.start()
    lat_shift, lon_shift = shift_ref[:, :1], shift_ref[:, 1:]
    n_rows, n_cols = pick_ref.shape
    n_tok = n_rows // 2
    row = iota((n_rows, 1), 0)
    level = row // (WIN * WIN) % (n_tok // (WIN * WIN))
    at_lat = row // WIN % WIN + lat_shift
    at_lon = row % WIN + row // n_tok * WIN + lon_shift
    cols, margin = 2 * WIN, WIN - 1
    starts = [sum(sizes[:i]) for i in range(len(sizes))]
    inside = (level * WIN + at_lat) * cols + at_lon
    north = (level * margin + at_lat - WIN) * WIN + at_lon % WIN
    east = (level * WIN + at_lat) * WIN + at_lon - cols
    index = jnp.where(
        at_lat < WIN,
        jnp.where(at_lon < cols, inside, east + starts[3]),
        north + jnp.where(at_lon < WIN, starts[1], jnp.where(at_lon < cols, starts[2], starts[4])),
    )
    pick_ref[...] = (index == iota((n_rows, n_cols), 1)).astype(BF16)
    copy.wait()


def enrich_body(n_lat, tok_ref, *refs):
    parts, (own_ref, north0_ref, north1_ref, east_ref) = refs[:n_lat], refs[n_lat:]
    _, levels, rows, cols, width = tok_ref.shape
    n_tok = levels * rows * cols
    half = width // 2
    tags = sum(part[:, width + half :].astype(F32) for part in parts).astype(jnp.int32)
    row = iota((n_tok, LANES), 0) + 1
    places = [(tags[i : i + 1] == row).astype(BF16)[:, : n_lat * TILE] for i in range(3)]
    got = jnp.concatenate([part[...] for part in parts], axis=0)
    extra = got[:, width : width + half]
    total = tok_ref[...].reshape(n_tok, width).astype(F32) + matmul(places[0], got[:, :width])
    total = total + jnp.concatenate([matmul(place, extra) for place in places[1:]], axis=1)
    own_ref[...] = total.astype(BF16)
    grid = total.reshape(levels, rows, cols, width)
    for out_ref, part in (
        (north0_ref, grid[:, : rows - 1, :WIN]),
        (north1_ref, grid[:, : rows - 1, WIN:]),
        (east_ref, grid[:, :, :WIN]),
    ):
        out_ref[...] = part.reshape(out_ref.shape).astype(BF16)


def region_body(pick_ref, gain_ref, *refs):
    sources, (region_ref, normed_ref) = refs[:-2], refs[-2:]
    region = matmul(pick_ref[...], jnp.concatenate([ref[...] for ref in sources], axis=0))
    region_ref[...] = region.astype(BF16)
    centred = region - jnp.mean(region, axis=-1, keepdims=True)
    variance = jnp.mean(centred * centred, axis=-1, keepdims=True)
    normed_ref[...] = (centred * lax.rsqrt(variance + 1e-05) * gain_ref[...]).astype(BF16)


def block_start(part, k, n_lat, n_dp, d_blk):
    lat = lax.axis_index("lat") + k
    lat = jnp.where(lat >= n_lat, lat - n_lat, lat)
    dp = lax.axis_index("dp")
    dp = 1 - dp if part else dp
    return pl.multiple_of((lat * n_dp + dp) * d_blk, d_blk)


def attend_body(part, turns, n_lat, n_dp, normed_ref, wqkv_ref, shift_ref, out_ref):
    n_rows, width = normed_ref.shape
    n_tok = n_rows // 2
    d_blk = width // (n_lat * n_dp)
    starts = [block_start(part, k, n_lat, n_dp, d_blk) for k in turns]
    normed = normed_ref[...]
    thirds = []
    for third in range(3):
        weights = jnp.concatenate(
            [wqkv_ref[:, pl.ds(third * width + at, d_blk)] for at in starts], axis=1
        )
        thirds.append(matmul(normed, weights))
    scale = (d_blk // 2) ** (-0.5)
    queries = (thirds[0].astype(BF16).astype(F32) * scale).astype(BF16)
    keys, values = thirds[1].astype(BF16), thirds[2].astype(BF16)
    key = iota((1, n_tok), 1)
    valid = lax.axis_index("lat") * WIN + key // WIN % WIN + shift_ref[:, :1] < WIN * n_lat
    first = iota((n_tok, d_blk), 1) < d_blk // 2
    ones, none = jnp.ones((n_tok, d_blk), BF16), jnp.zeros((n_tok, d_blk), BF16)
    units = [
        (slice(which * n_tok, (which + 1) * n_tok), slice(k * d_blk, (k + 1) * d_blk))
        for which in range(2)
        for k in range(len(turns))
    ]
    scores = []
    for unit in units:
        query = queries[unit]
        both = jnp.concatenate(
            [jnp.where(first, query, none), jnp.where(first, none, query)], axis=0
        )
        scores.append(
            lax.dot_general(both, keys[unit], (((1,), (1,)), ((), ())), preferred_element_type=F32)
        )
    scores = [jnp.where(valid, score, -1e30) for score in scores]
    highest = [jnp.max(score, axis=-1, keepdims=True) for score in scores]
    powers = [jnp.exp(score - top).astype(BF16) for score, top in zip(scores, highest)]
    mixed = [
        matmul(power, jnp.concatenate([values[unit], ones], axis=1))
        for power, unit in zip(powers, units)
    ]
    for context, unit in zip(mixed, units):
        context = context[:, :d_blk] / context[:, d_blk:]
        out_ref[unit] = jnp.where(first, context[:n_tok], context[n_tok:]).astype(BF16)


def turn_body(n_lon, cot_ref, other_ref, out_ref, flat_ref):
    _, levels, rows, cols, width = cot_ref.shape
    e_blk = width // n_lon
    n_tok = levels * rows * WIN
    here = lax.axis_index("lon")
    at = 0
    for ref in (cot_ref, other_ref):
        grid = ref[...].astype(F32).reshape(levels * rows, cols, width)
        for which in range(cols // WIN):
            flat_ref[...] = grid[:, which * WIN : (which + 1) * WIN].reshape(n_tok, width)
            for place, block in enumerate(reversed_order(n_lon)):
                lon = here ^ block
                piece = flat_ref[:, pl.ds(pl.multiple_of(lon * e_blk, e_blk), e_blk)]
                out_ref[place, :, at : at + n_tok] = piece.T.astype(BF16)
            at += n_tok


def reversed_order(count):
    bits = count.bit_length() - 1
    return [int(format(i, f"0{bits}b")[::-1], 2) if bits else 0 for i in range(count)]


def project_body(groups, n_lat, n_dp, reg_ref, wout_ref, *refs):
    ctx_refs, out_ref = refs[:-1], refs[-1]
    _, levels, rows, cols, width = out_ref.shape
    d_blk = width // (n_lat * n_dp)
    mixed = reg_ref[...].astype(F32)
    for (part, turns), ctx_ref in zip(groups, ctx_refs):
        starts = [block_start(part, k, n_lat, n_dp, d_blk) for k in turns]
        weights = jnp.concatenate([wout_ref[pl.ds(at, d_blk), :] for at in starts], axis=0)
        mixed = mixed + matmul(ctx_ref[...], weights)
    n_tok = levels * rows * WIN
    halves = [
        mixed[i * n_tok : (i + 1) * n_tok].reshape(levels * rows, WIN, width)
        for i in range(cols // WIN)
    ]
    out_ref[...] = jnp.concatenate(halves, axis=1).astype(BF16).reshape(out_ref.shape)


def gradient_body(cot_ref, mine_ref, other_ref, keep_ref, send_ref):
    context = jnp.concatenate([mine_ref[...], other_ref[...]], axis=0)
    count = cot_ref.shape[0] // 2
    for place in range(count):
        send_ref[place] = matmul(cot_ref[count + place], context).astype(BF16)
    for place in range(count):
        keep_ref[place] = matmul(cot_ref[place], context)


def in_hbm(array):
    return pltpu.with_memory_space_constraint(array, pltpu.HBM)


def fast_program(
    tokens, norm_gain, w_qkv, w_out, obs_vectors, obs_lat, obs_cell, obs_count, shift_offsets, cotangent
):
    _, levels, lat_dev, lon_dev, d_model = tokens.shape
    n_lat, n_lon, n_dp = (lax.axis_size(axis) for axis in ("lat", "lon", "dp"))
    shape = jax.ShapeDtypeStruct
    n_tok = levels * lat_dev * WIN
    n_rows = levels * lat_dev * lon_dev
    n_margin = levels * (lat_dev - 1) * WIN
    e_blk = d_model // n_lon
    d_blk = d_model // (n_lat * n_dp)
    dma = pltpu.SemaphoreType.DMA

    fetched = (obs_cell.reshape(1, -1), obs_lat.reshape(1, -1), obs_vectors)
    obs_rows = obs_vectors.shape[0]
    above = call(above_body, shape((obs_rows, obs_rows), BF16), (), [], "above", flops=SLOW)
    above, obs_count = lax.optimization_barrier((above, obs_count))
    live = call(
        live_body,
        shape(fetched[0].shape, jnp.int32),
        (obs_count,),
        [SMEM_SPEC],
        "live",
    )
    payload = call(
        functools.partial(route_body, n_lat),
        [shape((TILE, d_model + d_model // 2 + LANES), BF16)] * n_lat,
        (above, live, *fetched),
        [VMEM_SPEC] * 5,
        "route",
    )
    arrived = [payload[0]] + [shifted(payload[k], "lat", k) for k in range(1, n_lat)]

    sizes = (n_rows, n_margin, n_margin, n_tok, n_margin)
    shift_offsets, tokens = lax.optimization_barrier((payload[0], shift_offsets, tokens))[1:]
    tokens, picks = call(
        functools.partial(stage_body, sizes),
        [shape(tokens.shape, BF16), shape((n_rows, sum(sizes)), BF16)],
        (shift_offsets, in_hbm(tokens)),
        [VMEM_SPEC, ANY_SPEC],
        "stage",
        [dma],
    )
    own, north0, north1, east = call(
        functools.partial(enrich_body, n_lat),
        [shape((n, d_model), BF16) for n in (n_rows, n_margin, n_margin, n_tok)],
        (tokens, *arrived),
        [VMEM_SPEC] * (1 + n_lat),
        "enrich",
    )
    north0 = from_behind(north0, "lat", -1)
    north1 = from_behind(north1, "lat", -1)
    east = shifted(east, "lon", -1)
    cot_other = swapped(cotangent, "dp", 1)
    corner = shifted(north0, "lon", -1)
    loaded = (w_qkv, w_out, norm_gain.reshape(1, -1))
    loaded = lax.optimization_barrier((north0, *loaded))[1:]
    w_qkv, w_out, gain = load(loaded, "weights")
    region, normed = call(
        region_body,
        [shape((n_rows, d_model), BF16)] * 2,
        (picks, gain, own, north0, north1, east, corner),
        [VMEM_SPEC] * 7,
        "region",
    )
    first, second = [k for k in range(n_lat) if k % 3][::-1], [k for k in range(n_lat) if k % 3 == 0]

    def attend(normed, part, turns):
        return call(
            functools.partial(attend_body, part, turns, n_lat, n_dp),
            shape((n_rows, len(turns) * d_blk), BF16),
            (normed, w_qkv, shift_offsets),
            [VMEM_SPEC] * 3,
            f"attend{part}{turns[0]}",
            flops=SLOW if (part, turns) == (0, second) else 1,
        )

    def local_gradient(turns, mine, other, cost):
        width = len(turns) * d_blk
        return call(
            gradient_body,
            [shape((n_lon // 2, e_blk, width), F32), shape((n_lon // 2, e_blk, width), BF16)],
            (cot_turned, mine, other),
            [VMEM_SPEC] * 3,
            f"gradient{turns[0]}",
            flops=cost,
        )

    def halves(total):
        middle = total.shape[0] // 2
        return total[:middle], total[middle:].astype(BF16)

    def fold(kept, sent, bit):
        return kept + swapped(sent, "lon", bit).astype(F32)

    def over_lon(total, bit):
        while bit < n_lon:
            total = fold(*halves(total), bit)
            bit *= 2
        return total

    def over_lat(total, turns):
        blocks = []
        for i, k in enumerate(turns):
            block = total[..., i * d_blk : (i + 1) * d_blk]
            blocks.append(shifted(block.astype(BF16), "lat", k).astype(F32) if k else block)
        return functools.reduce(jnp.add, blocks)

    def after(array, *others):
        return lax.optimization_barrier((array, *others))[0]

    cot_turned = call(
        functools.partial(turn_body, n_lon),
        shape((n_lon, e_blk, n_dp * n_rows), BF16),
        (cotangent, cot_other),
        [VMEM_SPEC] * 2,
        "turn",
        [pltpu.VMEM((n_tok, d_model), F32)],
    )
    theirs0 = attend(normed, 1, first)
    got0 = swapped(theirs0, "dp", 1)
    mine0 = attend(after(normed, theirs0), 0, first)
    theirs1 = attend(after(normed, mine0), 1, second)
    got1 = swapped(theirs1, "dp", 1)
    kept0, sent0 = local_gradient(first, mine0, after(got0, theirs1), 1)
    mine1 = attend(after(normed, sent0), 0, second)
    kept0, sent0 = halves(fold(after(kept0, mine1), sent0, 1))
    kept1, sent1 = local_gradient(second, mine1, after(got1, sent0), SLOW)
    kept1, sent1 = halves(fold(kept1, sent1, 1))
    groups = [(1, first), (0, first), (1, second), (0, second)]
    block_out = call(
        functools.partial(project_body, groups, n_lat, n_dp),
        shape((1, levels, lat_dev, lon_dev, d_model), BF16),
        (after(region, sent0), w_out, theirs0, mine0, theirs1, mine1),
        [VMEM_SPEC] * 6,
        "project",
        flops=SLOW,
    )
    total0 = fold(after(kept0, block_out, sent1), sent0, 2)
    total1 = fold(kept1, sent1, 2)
    gradient = over_lat(over_lon(total0, 4), first)
    gradient, total1 = lax.optimization_barrier((gradient, over_lat(over_lon(total1, 4), second)))
    gradient = (gradient + total1)[0]
    return (block_out, gradient)


def on_device(tokens, norm_gain, w_qkv, w_out, obs_vectors, *rest):
    _, _, lat_dev, lon_dev, d_model = tokens.shape
    n_lat, n_lon, n_dp = (lax.axis_size(axis) for axis in ("lat", "lon", "dp"))
    cap = obs_vectors.shape[0] * 3 // (2 * n_lat)
    fits = (
        n_dp == 2
        and n_lon > 2
        and n_lon & (n_lon - 1) == 0
        and n_lat * TILE <= LANES
        and n_lat <= TILE
        and cap * 2 == TILE * 3
        and lat_dev == WIN
        and lon_dev == 2 * WIN
        and d_model // n_lon % LANES == 0
        and d_model // (n_lat * n_dp) == LANES
        and d_model // HEADS * 2 == LANES
    )
    program = fast_program if fits else general_program
    return program(tokens, norm_gain, w_qkv, w_out, obs_vectors, *rest)


def solution(mesh):
    placed = (
        P("dp", None, "lat", "lon", None),
        P(),
        P(),
        P(),
        P(("lon", "lat", "dp"), None),
        P(("lon", "lat", "dp"), None),
        P(("lon", "lat", "dp")),
        P(("lon", "lat", "dp")),
        P("dp", None),
        P("dp", None, "lat", "lon", None),
    )
    return jax.shard_map(
        on_device,
        mesh=mesh,
        in_specs=placed,
        out_specs=(P("dp", None, "lat", "lon", None), P("lon", ("lat", "dp"))),
        check_vma=False,
    )
```
